32 devices in a mesh: slab: 4 (over y, x), angle: 8 (over z, core).
Axes of the slice: x: 2, y: 2, z: 4, core: 2. Of those that a mesh axis runs over, the one named last changes fastest.
Arguments:
- volume: bfloat16 [32, 32, 2048], P('slab', 'angle'), may hold values from -6 to 6
- measured: float32 [8, 32, 2048], P('angle', 'slab'), may hold values from -6 to 6
- ray_tiles: bfloat16 [8, 32, 2, 128, 128], P(None, 'angle'), may hold values from -0.0625 to 0.0625
- tile_offsets: int32 [8, 32], replicated, may hold values from -3 to 3
- band_counts: int32 [8, 32], replicated, may hold values from 1 to 2
Outputs:
- updated: float32 [32, 32, 2048], P('slab', 'angle')
- residual: float32 [8, 32, 2048], P('angle', 'slab')
The draws below stay inside these ranges and needn't reach their ends.
All inputs are finite; a program needn't handle non-finite values.
Results may differ from the reference program's by a relative error of at most 0.00056.
Values may be sent and summed in bfloat16 or wider, within the bound.
A program may use at most 64 MiB of HBM per device.

```python
import jax
import jax.numpy as jnp
from jax import lax

NX = 2048
TILE = 128
BAND = 2
OFFMAX = 3
NZ = 32
NY = 32
SUBSET = 8


def with_ends(array, own_key, smallest, high):
    longest = array.shape.index(max(array.shape))
    spots = []
    for shift in (0, 1):
        where = [jax.random.randint(jax.random.fold_in(own_key, axis), (), 0, length) for axis, length in enumerate(array.shape)]
        where[longest] = (where[longest] + shift) % array.shape[longest]
        spots.append(tuple(where))
    return array.at[spots[0]].set(smallest).at[spots[1]].set(high)


def steps_of(rng, extent, pieces, smallest, high):
    loudness = 1.0
    for dim, shards_of in pieces:
        steps = jax.random.uniform(jax.random.fold_in(jax.random.fold_in(rng, 6), dim), (shards_of,), jnp.float32, smallest / len(pieces), high / len(pieces))
        loudness = loudness * jnp.repeat(jnp.exp(steps), extent[dim] // shards_of).reshape((-1,) + (1,) * (len(extent) - 1 - dim))
    return loudness


def bell_draw(key, extent, scale, limit, pieces=(), kind=jnp.bfloat16):
    entries = jax.random.normal(key, extent, jnp.float32) * scale
    if len(pieces) > 0:
        entries = steps_of(key, extent, pieces, -0.22, 0.18) * entries
    return jnp.clip(entries, min=-limit, max=limit).astype(kind)


def setup_inputs(seed: int = 0) -> dict:
    keys = jax.random.split(jax.random.key(seed), 6)
    return {
        "volume": bell_draw(keys[0], (NZ, NY, NX), 1.0, 6.0, ((0, 4), (1, 8))),
        "measured": bell_draw(keys[1], (SUBSET, NZ, NX), 1.0, 6.0, ((0, 8), (1, 4)), jnp.float32),
        "ray_tiles": bell_draw(keys[2], (SUBSET, NY, BAND, TILE, TILE), (NY * BAND * TILE) ** -0.5, 0.0625, ((1, 8),)),
        "tile_offsets": with_ends(jax.random.randint(keys[3], (SUBSET, NY), 0 - OFFMAX, OFFMAX + 1), jax.random.fold_in(keys[3], 1), 0 - OFFMAX, OFFMAX).astype(jnp.int32),
        "band_counts": with_ends(jax.random.randint(keys[4], (SUBSET, NY), 1, BAND + 1), jax.random.fold_in(keys[4], 1), 1, BAND).astype(jnp.int32),
    }


step_size = 0.3
smooth_weight = 0.2
smooth_floor = 0.25

def shift_table(tile_offsets, band_counts, band):
    center = band // 2
    shifts = jnp.stack([tile_offsets + (k - center) for k in range(band)], axis=1).astype(jnp.int32)
    masks = jnp.stack([band_counts > k for k in range(band)], axis=1).astype(jnp.bfloat16)
    return (shifts, masks)

def project_angle(padded, shifts, masks, tiles, margin):
    tile_count = padded.shape[2] - 2 * margin
    summed = jnp.zeros((padded.shape[0], tile_count, padded.shape[3]), jnp.float32)
    for k in range(tiles.shape[1]):
        moved = jax.vmap(lambda block, offset: lax.dynamic_slice_in_dim(block, (margin + offset).astype(jnp.int32), tile_count, 1), in_axes=(1, 0), out_axes=1)(padded, shifts[k])
        moved = moved * masks[k][None, :, None, None]
        summed = summed + jnp.einsum('zrtc,rcd->ztd', moved.astype(jnp.float32), tiles[:, k].astype(jnp.float32))
    return summed.reshape(padded.shape[0], tile_count * padded.shape[3])

def spread_angle(view_pad, shifts, masks, tiles, margin):
    tile_count = view_pad.shape[1] - 2 * margin
    rows_here = shifts.shape[1]
    summed = jnp.zeros((view_pad.shape[0], rows_here, tile_count, view_pad.shape[2]), jnp.float32)
    for k in range(tiles.shape[1]):
        moved = jax.vmap(lambda offset: lax.dynamic_slice_in_dim(view_pad, (margin - offset).astype(jnp.int32), tile_count, 1), out_axes=1)(shifts[k])
        product = jnp.einsum('zrtd,rcd->zrtc', moved.astype(jnp.float32), tiles[:, k].astype(jnp.float32))
        summed = summed + product * masks[k].astype(jnp.float32)[None, :, None, None]
    return summed.reshape(view_pad.shape[0], rows_here, tile_count * view_pad.shape[2])

def divergence(field):
    base = field[:-1, :-1, :-1]
    step_z = field[1:, :-1, :-1] - base
    step_y = field[:-1, 1:, :-1] - base
    step_x = field[:-1, :-1, 1:] - base
    scale = jnp.sqrt(step_z * step_z + step_y * step_y + step_x * step_x + smooth_floor)
    flow_z = step_z / scale
    flow_y = step_y / scale
    flow_x = step_x / scale
    result = flow_z[1:, 1:, 1:] - flow_z[:-1, 1:, 1:]
    result = result + flow_y[1:, 1:, 1:] - flow_y[1:, :-1, 1:]
    return result + flow_x[1:, 1:, 1:] - flow_x[1:, 1:, :-1]

def reference(volume, measured, ray_tiles, tile_offsets, band_counts):
    depth, rows_all, width = volume.shape
    band = ray_tiles.shape[2]
    tile = ray_tiles.shape[3]
    margin = OFFMAX + band
    tile_count = width // tile
    shifts, masks = shift_table(tile_offsets, band_counts, band)
    blocks = volume.reshape(depth, rows_all, tile_count, tile)
    padded = jnp.pad(blocks, ((0, 0), (0, 0), (margin, margin), (0, 0)))

    def one_view(items):
        return project_angle(padded, items[0], items[1], items[2], margin)
    views = lax.map(one_view, (shifts, masks, ray_tiles))
    residual = views - measured
    rounded = residual.astype(jnp.bfloat16)
    view_blocks = rounded.reshape(rounded.shape[0], depth, tile_count, tile)
    view_pad = jnp.pad(view_blocks, ((0, 0), (0, 0), (margin, margin), (0, 0)))

    def accumulate(carry, items):
        return (carry + spread_angle(items[0], items[1], items[2], items[3], margin), None)
    gradient, unused = lax.scan(accumulate, jnp.zeros((depth, rows_all, width), jnp.float32), (view_pad, shifts, masks, ray_tiles))
    field = jnp.pad(volume.astype(jnp.float32), 1)
    updated = volume.astype(jnp.float32) - step_size * gradient + step_size * smooth_weight * divergence(field)
    return (updated, residual)
```

```python
import functools

import jax
import jax.numpy as jnp
from jax import lax
from jax.experimental import pallas as pl
from jax.experimental.pallas import tpu as pltpu
from jax.sharding import PartitionSpec as P

OFFMAX = 3

step_size = 0.3
smooth_weight = 0.2
smooth_floor = 0.25

F32 = jnp.float32
BF16 = jnp.bfloat16


def kernel(
    slabs,
    n,
    vol_hbm,
    meas_hbm,
    tiles_hbm,
    off_ref,
    cnt_ref,
    upd_ref,
    res_ref,
    vol_in,
    meas,
    tiles,
    vol32,
    volt,
    part_own,
    sib_send,
    sib_recv,
    chip_send,
    chip_recv,
    same_recv,
    sibres_recv,
    own_res,
    respad,
    grad,
    base,
    flow_low,
    ys,
    yr,
    zr,
    cr,
    load_sem,
    sib_ssem,
    sib_rsem,
    chip_ssem,
    chip_rsem,
    same_ssem,
    same_rsem,
    sr_ssem,
    sr_rsem,
    y_ssem,
    y_rsem,
    z_ssem,
    z_rsem,
    c_ssem,
    c_rsem,
):
    depth, rows, width = vol_in.shape
    band = tiles.shape[2]
    tile = tiles.shape[3]
    tcount = width // tile
    flat = tcount * depth
    center = band // 2
    margin = OFFMAX + band
    zero_start = margin + tcount
    chips = n // 2

    slab = lax.axis_index("slab")
    me = lax.axis_index("angle")
    chip = lax.div(me, 2)
    core = lax.rem(me, 2)
    sib = me + 1 - 2 * core
    far_y = me - 1 + 2 * core
    first_row = me * rows
    barrier = pltpu.get_barrier_semaphore()

    has_far = (far_y >= 0) & (far_y < n)
    has_zp = slab + 1 < slabs
    has_zm = slab >= 1
    has_yp = me + 1 < n
    has_ym = me >= 1
    has_up = has_zp & has_ym
    has_down = has_zm & has_yp

    def greet(s, a):
        pl.semaphore_signal(barrier, inc=1, device_id=(s, a), device_id_type=pl.DeviceIdType.MESH)

    greet(slab, sib)
    for j in range(1, chips):
        greet(slab, 2 * lax.rem(chip + j, chips) + core)

    pl.when(has_far)(lambda: greet(slab, far_y))
    pl.when(has_zp)(lambda: greet(slab + 1, me))
    pl.when(has_zm)(lambda: greet(slab - 1, me))
    pl.when(has_up)(lambda: greet(slab + 1, me - 1))
    pl.when(has_down)(lambda: greet(slab - 1, me + 1))

    vol_copy = pltpu.make_async_copy(vol_hbm, vol_in, load_sem.at[0])
    vol_copy.start()
    order = [chips // 2] + [j for j in range(1, chips) if j != chips // 2] + [0]
    dest = [lax.rem(chip + j, chips) for j in order]
    loads = []
    for i in range(chips):
        pair = []
        for angle, slot in ((2 * dest[i] + 1 - core, 0), (2 * dest[i] + core, 1)):
            copy = pltpu.make_async_copy(
                tiles_hbm.at[angle], tiles.at[angle], load_sem.at[2 + 2 * i + slot]
            )
            copy.start()
            pair.append(copy)
        loads.append(pair)
    meas_copy = pltpu.make_async_copy(meas_hbm, meas, load_sem.at[1])
    meas_copy.start()

    volt[:, :margin] = jnp.zeros((rows, margin, depth, tile), F32)
    volt[:, zero_start:] = jnp.zeros((rows, volt.shape[1] - zero_start, depth, tile), F32)
    respad[:, :margin] = jnp.zeros((2, margin, depth, tile), F32)
    respad[:, zero_start:] = jnp.zeros((2, respad.shape[1] - zero_start, depth, tile), F32)
    vol_copy.wait()
    vol32[...] = vol_in[...].astype(F32)
    for y in range(rows):
        for t in range(tcount):
            volt[y, margin + t] = vol32[:, y, t * tile : (t + 1) * tile]

    def own_row(y):
        return volt[y, margin : margin + tcount].reshape(flat, tile)

    ys[0] = own_row(0).astype(BF16)
    ys[1] = own_row(rows - 1).astype(BF16)

    def send(src, dst, ssem, rsem, s, a):
        return pltpu.make_async_remote_copy(
            src_ref=src,
            dst_ref=dst,
            send_sem=ssem,
            recv_sem=rsem,
            device_id=(s, a),
            device_id_type=pl.DeviceIdType.MESH,
        )

    one = jnp.int32(1)
    none = jnp.int32(0)
    expect = jnp.int32(chips)
    for there in (has_far, has_zp, has_zm, has_up, has_down):
        expect = expect + jnp.where(there, one, none)
    pl.semaphore_wait(barrier, expect)

    halos = (
        (has_ym, send(ys.at[0], yr.at[1], y_ssem.at[0], y_rsem.at[1], slab, me - 1)),
        (has_yp, send(ys.at[1], yr.at[0], y_ssem.at[1], y_rsem.at[0], slab, me + 1)),
        (has_zm, send(vol32.at[0], zr.at[1], z_ssem.at[0], z_rsem.at[1], slab - 1, me)),
        (has_zp, send(vol32.at[depth - 1], zr.at[0], z_ssem.at[1], z_rsem.at[0], slab + 1, me)),
        (has_down, send(vol32.at[0], cr.at[1], c_ssem.at[0], c_rsem.at[1], slab - 1, me + 1)),
        (has_up, send(vol32.at[depth - 1], cr.at[0], c_ssem.at[1], c_rsem.at[0], slab + 1, me - 1)),
    )
    arrivals = (
        (has_yp, yr.at[1], send(ys.at[0], yr.at[1], y_ssem.at[0], y_rsem.at[1], slab, me + 1)),
        (has_ym, yr.at[0], send(ys.at[1], yr.at[0], y_ssem.at[1], y_rsem.at[0], slab, me - 1)),
        (has_zp, zr.at[1], send(vol32.at[0], zr.at[1], z_ssem.at[0], z_rsem.at[1], slab + 1, me)),
        (has_zm, zr.at[0], send(vol32.at[depth - 1], zr.at[0], z_ssem.at[1], z_rsem.at[0], slab - 1, me)),
        (has_up, cr.at[1], send(vol32.at[0], cr.at[1], c_ssem.at[0], c_rsem.at[1], slab + 1, me - 1)),
        (has_down, cr.at[0], send(vol32.at[depth - 1], cr.at[0], c_ssem.at[1], c_rsem.at[0], slab - 1, me + 1)),
    )
    for there, copy in halos:
        pl.when(there)(copy.start)

    def starts(angle, y, sign):
        found = []
        for k in range(band):
            shift = off_ref[angle, first_row + y] + (k - center)
            used = cnt_ref[angle, first_row + y] > k
            found.append(jnp.where(used, margin + sign * shift, zero_start))
        return found

    def view(angle):
        pieces = []
        for y in range(rows):
            for start in starts(angle, y, 1):
                pieces.append(volt[y, pl.ds(start, tcount)].reshape(flat, tile).astype(BF16))
        weights = tiles[angle].reshape(rows * band * tile, tile)
        return jnp.dot(jnp.concatenate(pieces, axis=1), weights, preferred_element_type=F32)

    def sib_copy(i):
        return send(sib_send.at[i], sib_recv.at[i], sib_ssem.at[i], sib_rsem.at[i], slab, sib)

    def chip_copy(i):
        return send(
            chip_send.at[i], chip_recv.at[i], chip_ssem.at[i], chip_rsem.at[i], slab, 2 * dest[i] + core
        )

    def for_sibling(i):
        loads[i][0].wait()
        sib_send[i] = view(2 * dest[i] + 1 - core)
        sib_copy(i).start()

    for_sibling(0)
    for i in range(chips):
        if i + 1 < chips:
            for_sibling(i + 1)
        loads[i][1].wait()
        part_own[...] = view(2 * dest[i] + core)
        sib_copy(i).wait_recv()
        if i + 1 < chips:
            chip_send[i] = part_own[...] + sib_recv[i]
            chip_copy(i).start()
        else:
            part_own[...] = part_own[...] + sib_recv[i]

    for there, buffer, copy in arrivals:
        pl.when(there)(copy.wait_recv)

        @pl.when(jnp.logical_not(there))
        def _(buffer=buffer):
            buffer[...] = jnp.zeros(buffer.shape, buffer.dtype)

    lane = lax.broadcasted_iota(jnp.int32, (flat + depth, tile), 1)
    level = lax.rem(lax.broadcasted_iota(jnp.int32, (flat + depth, tile), 0), depth)
    zeros_tile = jnp.zeros((depth, tile), F32)

    low = zr[0]
    low_y = jnp.concatenate([low[1:], cr[0][:1]], axis=0)
    low_lane = lax.broadcasted_iota(jnp.int32, (rows, width), 1)
    low_x = jnp.where(low_lane == width - 1, 0.0, pltpu.roll(low, width - 1, 1))
    lz, ly, lx = vol32[0] - low, low_y - low, low_x - low
    flow_low[...] = lz * lax.rsqrt(lz * lz + ly * ly + lx * lx + smooth_floor)

    def field_row(y):
        if 0 <= y < rows:
            return volt[y, margin - 1 : margin + tcount + 1].reshape(flat + 2 * depth, tile)
        inner = yr[0 if y < 0 else 1].astype(F32)
        return jnp.concatenate([zeros_tile, inner, zeros_tile], axis=0)

    def spread_row(ref, row):
        return [
            jnp.broadcast_to(ref[row : row + 1, t * tile : (t + 1) * tile], (depth, tile))
            for t in range(tcount)
        ]

    def flow(y):
        wide = field_row(y)
        here = wide[: flat + depth]
        rolled = pltpu.roll(wide, tile - 1, 1)
        dx = jnp.where(lane == tile - 1, rolled[depth:], rolled[: flat + depth]) - here
        dy = field_row(y + 1)[: flat + depth] - here
        top = spread_row(zr.at[1], y) if y >= 0 else spread_row(cr.at[1], rows - 1)
        top = jnp.concatenate([zeros_tile] + top, axis=0)
        dz = jnp.where(level == depth - 1, top, pltpu.roll(here, flat + depth - 1, 0)) - here
        inv = lax.rsqrt(dz * dz + dy * dy + dx * dx + smooth_floor)
        return dz * inv, dy * inv, dx * inv

    before = flow(-1)[1][depth:]
    for y in range(rows):
        fz, fy, fx = flow(y)
        fz, fy = fz[depth:], fy[depth:]
        under = jnp.concatenate(spread_row(flow_low, y), axis=0)
        div = fz - jnp.where(level[:flat] == 0, under, pltpu.roll(fz, 1, 0))
        div = div + (fy - before)
        rolled = pltpu.roll(fx, 1, 1)
        div = div + (fx[depth:] - jnp.where(lane[:flat] == 0, rolled[:flat], rolled[depth:]))
        base[y] = own_row(y) + step_size * smooth_weight * div
        before = fy

    total = part_own[...]
    for i in range(chips - 1):
        chip_copy(i).wait_recv()
        total = total + chip_recv[i]
    meas_copy.wait()
    total = total.reshape(tcount, depth, tile)
    for t in range(tcount):
        here = total[t] - meas[0, :, t * tile : (t + 1) * tile]
        res_ref[0, :, t * tile : (t + 1) * tile] = here
        respad[0, margin + t] = here.astype(BF16).astype(F32)
    own_res[...] = respad[0, margin:zero_start].reshape(flat, tile).astype(BF16)

    def same_copy(i):
        return send(own_res, same_recv.at[i], same_ssem.at[i], same_rsem.at[i], slab, 2 * dest[i] + core)

    def forward(i):
        src = own_res if i == chips - 1 else same_recv.at[i]
        return send(src, sibres_recv.at[i], sr_ssem.at[i], sr_rsem.at[i], slab, sib)

    for i in range(chips - 1):
        same_copy(i).start()
    forward(chips - 1).start()

    def back(angle, slot, fresh):
        for y in range(rows):
            acc = None
            for k, start in enumerate(starts(angle, y, -1)):
                piece = respad[slot, pl.ds(start, tcount)].reshape(flat, tile).astype(BF16)
                product = lax.dot_general(
                    piece, tiles[angle, y, k], (((1,), (1,)), ((), ())), preferred_element_type=F32
                )
                acc = product if acc is None else acc + product
            grad[y] = acc if fresh else grad[y] + acc

    def take(block, slot):
        respad[slot, margin:zero_start] = block.astype(F32).reshape(tcount, depth, tile)

    back(me, 0, True)
    forward(chips - 1).wait_recv()
    take(sibres_recv[chips - 1], 1)
    back(sib, 1, False)
    for i in range(chips - 1):
        source = lax.rem(chip + chips - order[i], chips)
        same_copy(i).wait_recv()
        forward(i).start()
        take(same_recv[i], 0)
        back(2 * source + core, 0, False)
        forward(i).wait_recv()
        take(sibres_recv[i], 1)
        back(2 * source + 1 - core, 1, False)

    for y in range(rows):
        out = (base[y] - step_size * grad[y]).reshape(tcount, depth, tile)
        for t in range(tcount):
            upd_ref[:, y, t * tile : (t + 1) * tile] = out[t]

    for there, copy in halos:
        pl.when(there)(copy.wait_send)
    for i in range(chips):
        sib_copy(i).wait_send()
        forward(i).wait_send()
    for i in range(chips - 1):
        chip_copy(i).wait_send()
        same_copy(i).wait_send()


def per_device(slabs, n, volume, measured, ray_tiles, tile_offsets, band_counts):
    depth, rows, width = volume.shape
    count, unused, band, tile, unused_2 = ray_tiles.shape
    tcount = width // tile
    flat = tcount * depth
    padded = 2 * tcount + OFFMAX + band
    chips = n // 2
    dma = pltpu.SemaphoreType.DMA
    vmem = pltpu.VMEM
    block = (flat, tile)
    return pl.pallas_call(
        functools.partial(kernel, slabs, n),
        out_shape=(
            jax.ShapeDtypeStruct(volume.shape, F32),
            jax.ShapeDtypeStruct(measured.shape, F32),
        ),
        in_specs=[pl.BlockSpec(memory_space=pl.ANY)] * 3
        + [pl.BlockSpec(memory_space=pltpu.SMEM)] * 2,
        out_specs=(pl.BlockSpec(memory_space=pltpu.VMEM),) * 2,
        scratch_shapes=[
            vmem(volume.shape, BF16),
            vmem(measured.shape, F32),
            vmem(ray_tiles.shape, BF16),
            vmem(volume.shape, F32),
            vmem((rows, padded, depth, tile), F32),
            vmem(block, F32),
            vmem((chips, *block), F32),
            vmem((chips, *block), F32),
            vmem((chips - 1, *block), F32),
            vmem((chips - 1, *block), F32),
            vmem((chips - 1, *block), BF16),
            vmem((chips, *block), BF16),
            vmem(block, BF16),
            vmem((2, padded, depth, tile), F32),
            vmem((rows, *block), F32),
            vmem((rows, *block), F32),
            vmem((rows, width), F32),
            vmem((2, *block), BF16),
            vmem((2, *block), BF16),
            vmem((2, rows, width), F32),
            vmem((2, rows, width), F32),
            dma((2 + n,)),
            dma((chips,)),
            dma((chips,)),
            dma((chips - 1,)),
            dma((chips - 1,)),
            dma((chips - 1,)),
            dma((chips - 1,)),
            dma((chips,)),
            dma((chips,)),
            dma((2,)),
            dma((2,)),
            dma((2,)),
            dma((2,)),
            dma((2,)),
            dma((2,)),
        ],
        compiler_params=pltpu.CompilerParams(
            collective_id=0, has_side_effects=True, vmem_limit_bytes=40 * 1024 * 1024
        ),
        name="step",
    )(volume, measured, ray_tiles, tile_offsets, band_counts)


def solution(mesh):
    return jax.shard_map(
        functools.partial(per_device, mesh.shape["slab"], mesh.shape["angle"]),
        mesh=mesh,
        in_specs=(
            P("slab", "angle", None),
            P("angle", "slab", None),
            P(None, "angle", None, None, None),
            P(),
            P(),
        ),
        out_specs=(P("slab", "angle", None), P("angle", "slab", None)),
        check_vma=False,
    )
```

```python
import functools

import jax
import jax.numpy as jnp
from jax import lax
from jax.experimental import pallas as pl
from jax.experimental.pallas import tpu as pltpu
from jax.sharding import PartitionSpec as P

OFFMAX = 3

step_size = 0.3
smooth_weight = 0.2
smooth_floor = 0.25

F32 = jnp.float32
BF16 = jnp.bfloat16


def kernel(
    slabs,
    n,
    vol_hbm,
    meas_hbm,
    tiles_hbm,
    off_hbm,
    cnt_hbm,
    upd_ref,
    res_ref,
    vol_in,
    meas,
    tiles,
    vol32,
    volt,
    part_own,
    sib_send,
    sib_recv,
    chip_send,
    chip_recv,
    same_recv,
    sibres_recv,
    own_res,
    respad,
    grad,
    base,
    flow_low,
    ys,
    yr,
    zr,
    cr,
    off_ref,
    cnt_ref,
    load_sem,
    sib_ssem,
    sib_rsem,
    chip_ssem,
    chip_rsem,
    same_ssem,
    same_rsem,
    sr_ssem,
    sr_rsem,
    y_ssem,
    y_rsem,
    z_ssem,
    z_rsem,
    c_ssem,
    c_rsem,
):
    depth, rows, width = vol_in.shape
    band = tiles.shape[2]
    tile = tiles.shape[3]
    tcount = width // tile
    flat = tcount * depth
    center = band // 2
    margin = OFFMAX + band
    zero_start = margin + tcount
    chips = n // 2

    slab = lax.axis_index("slab")
    me = lax.axis_index("angle")
    chip = lax.div(me, 2)
    core = lax.rem(me, 2)
    sib = me + 1 - 2 * core
    far_y = me - 1 + 2 * core
    first_row = me * rows
    barrier = pltpu.get_barrier_semaphore()

    has_far = (far_y >= 0) & (far_y < n)
    has_zp = slab + 1 < slabs
    has_zm = slab >= 1
    has_yp = me + 1 < n
    has_ym = me >= 1
    has_up = has_zp & has_ym
    has_down = has_zm & has_yp

    def greet(s, a):
        pl.semaphore_signal(barrier, inc=1, device_id=(s, a), device_id_type=pl.DeviceIdType.MESH)

    greet(slab, sib)
    for j in range(1, chips):
        greet(slab, 2 * lax.rem(chip + j, chips) + core)

    pl.when(has_far)(lambda: greet(slab, far_y))
    pl.when(has_zp)(lambda: greet(slab + 1, me))
    pl.when(has_zm)(lambda: greet(slab - 1, me))
    pl.when(has_up)(lambda: greet(slab + 1, me - 1))
    pl.when(has_down)(lambda: greet(slab - 1, me + 1))

    vol_copy = pltpu.make_async_copy(vol_hbm, vol_in, load_sem.at[0])
    vol_copy.start()
    off_copy = pltpu.make_async_copy(off_hbm, off_ref, load_sem.at[n + 2])
    off_copy.start()
    cnt_copy = pltpu.make_async_copy(cnt_hbm, cnt_ref, load_sem.at[n + 3])
    cnt_copy.start()
    order = [chips // 2] + [j for j in range(1, chips) if j != chips // 2] + [0]
    dest = [lax.rem(chip + j, chips) for j in order]
    loads = []
    for i in range(chips):
        pair = []
        for angle, slot in ((2 * dest[i] + 1 - core, 0), (2 * dest[i] + core, 1)):
            copy = pltpu.make_async_copy(
                tiles_hbm.at[angle], tiles.at[angle], load_sem.at[2 + 2 * i + slot]
            )
            copy.start()
            pair.append(copy)
        loads.append(pair)
    meas_copy = pltpu.make_async_copy(meas_hbm, meas, load_sem.at[1])
    meas_copy.start()

    volt[:, :margin] = jnp.zeros((rows, margin, depth, tile), F32)
    volt[:, zero_start:] = jnp.zeros((rows, volt.shape[1] - zero_start, depth, tile), F32)
    respad[:, :margin] = jnp.zeros((2, margin, depth, tile), F32)
    respad[:, zero_start:] = jnp.zeros((2, respad.shape[1] - zero_start, depth, tile), F32)
    vol_copy.wait()
    vol32[...] = vol_in[...].astype(F32)
    for y in range(rows):
        for t in range(tcount):
            volt[y, margin + t] = vol32[:, y, t * tile : (t + 1) * tile]

    def own_row(y):
        return volt[y, margin : margin + tcount].reshape(flat, tile)

    ys[0] = own_row(0).astype(BF16)
    ys[1] = own_row(rows - 1).astype(BF16)

    def send(src, dst, ssem, rsem, s, a):
        return pltpu.make_async_remote_copy(
            src_ref=src,
            dst_ref=dst,
            send_sem=ssem,
            recv_sem=rsem,
            device_id=(s, a),
            device_id_type=pl.DeviceIdType.MESH,
        )

    halos = (
        (has_ym, send(ys.at[0], yr.at[1], y_ssem.at[0], y_rsem.at[1], slab, me - 1)),
        (has_yp, send(ys.at[1], yr.at[0], y_ssem.at[1], y_rsem.at[0], slab, me + 1)),
        (has_zm, send(vol32.at[0], zr.at[1], z_ssem.at[0], z_rsem.at[1], slab - 1, me)),
        (has_zp, send(vol32.at[depth - 1], zr.at[0], z_ssem.at[1], z_rsem.at[0], slab + 1, me)),
        (has_down, send(vol32.at[0], cr.at[1], c_ssem.at[0], c_rsem.at[1], slab - 1, me + 1)),
        (has_up, send(vol32.at[depth - 1], cr.at[0], c_ssem.at[1], c_rsem.at[0], slab + 1, me - 1)),
    )
    arrivals = (
        (has_yp, yr.at[1], send(ys.at[0], yr.at[1], y_ssem.at[0], y_rsem.at[1], slab, me + 1)),
        (has_ym, yr.at[0], send(ys.at[1], yr.at[0], y_ssem.at[1], y_rsem.at[0], slab, me - 1)),
        (has_zp, zr.at[1], send(vol32.at[0], zr.at[1], z_ssem.at[0], z_rsem.at[1], slab + 1, me)),
        (has_zm, zr.at[0], send(vol32.at[depth - 1], zr.at[0], z_ssem.at[1], z_rsem.at[0], slab - 1, me)),
        (has_up, cr.at[1], send(vol32.at[0], cr.at[1], c_ssem.at[0], c_rsem.at[1], slab + 1, me - 1)),
        (has_down, cr.at[0], send(vol32.at[depth - 1], cr.at[0], c_ssem.at[1], c_rsem.at[0], slab - 1, me + 1)),
    )
    def starts(angle, y, sign):
        found = []
        for k in range(band):
            shift = off_ref[angle, first_row + y] + (k - center)
            used = cnt_ref[angle, first_row + y] > k
            found.append(jnp.where(used, margin + sign * shift, zero_start))
        return found

    def view(angle):
        pieces = []
        for y in range(rows):
            for start in starts(angle, y, 1):
                pieces.append(volt[y, pl.ds(start, tcount)].reshape(flat, tile).astype(BF16))
        weights = tiles[angle].reshape(rows * band * tile, tile)
        return jnp.dot(jnp.concatenate(pieces, axis=1), weights, preferred_element_type=F32)

    def sib_copy(i):
        return send(sib_send.at[i], sib_recv.at[i], sib_ssem.at[i], sib_rsem.at[i], slab, sib)

    def chip_copy(i):
        return send(
            chip_send.at[i], chip_recv.at[i], chip_ssem.at[i], chip_rsem.at[i], slab, 2 * dest[i] + core
        )

    def for_sibling(i):
        loads[i][0].wait()
        sib_send[i] = view(2 * dest[i] + 1 - core)

    off_copy.wait()
    cnt_copy.wait()
    for_sibling(0)

    one = jnp.int32(1)
    none = jnp.int32(0)
    expect = jnp.int32(chips)
    for there in (has_far, has_zp, has_zm, has_up, has_down):
        expect = expect + jnp.where(there, one, none)
    pl.semaphore_wait(barrier, expect)

    sib_copy(0).start()
    for there, copy in halos:
        pl.when(there)(copy.start)

    for i in range(chips):
        if i + 1 < chips:
            for_sibling(i + 1)
            sib_copy(i + 1).start()
        loads[i][1].wait()
        part_own[...] = view(2 * dest[i] + core)
        sib_copy(i).wait_recv()
        if i + 1 < chips:
            chip_send[i] = part_own[...] + sib_recv[i]
            chip_copy(i).start()
        else:
            part_own[...] = part_own[...] + sib_recv[i]

    for there, buffer, copy in arrivals:
        pl.when(there)(copy.wait_recv)

        @pl.when(jnp.logical_not(there))
        def _(buffer=buffer):
            buffer[...] = jnp.zeros(buffer.shape, buffer.dtype)

    lane = lax.broadcasted_iota(jnp.int32, (flat + depth, tile), 1)
    level = lax.rem(lax.broadcasted_iota(jnp.int32, (flat + depth, tile), 0), depth)
    zeros_tile = jnp.zeros((depth, tile), F32)

    low = zr[0]
    low_y = jnp.concatenate([low[1:], cr[0][:1]], axis=0)
    low_lane = lax.broadcasted_iota(jnp.int32, (rows, width), 1)
    low_x = jnp.where(low_lane == width - 1, 0.0, pltpu.roll(low, width - 1, 1))
    lz, ly, lx = vol32[0] - low, low_y - low, low_x - low
    flow_low[...] = lz * lax.rsqrt(lz * lz + ly * ly + lx * lx + smooth_floor)

    def field_row(y):
        if 0 <= y < rows:
            return volt[y, margin - 1 : margin + tcount + 1].reshape(flat + 2 * depth, tile)
        inner = yr[0 if y < 0 else 1].astype(F32)
        return jnp.concatenate([zeros_tile, inner, zeros_tile], axis=0)

    def spread_row(ref, row):
        return [
            jnp.broadcast_to(ref[row : row + 1, t * tile : (t + 1) * tile], (depth, tile))
            for t in range(tcount)
        ]

    def flow(y):
        wide = field_row(y)
        here = wide[: flat + depth]
        rolled = pltpu.roll(wide, tile - 1, 1)
        dx = jnp.where(lane == tile - 1, rolled[depth:], rolled[: flat + depth]) - here
        dy = field_row(y + 1)[: flat + depth] - here
        top = spread_row(zr.at[1], y) if y >= 0 else spread_row(cr.at[1], rows - 1)
        top = jnp.concatenate([zeros_tile] + top, axis=0)
        dz = jnp.where(level == depth - 1, top, pltpu.roll(here, flat + depth - 1, 0)) - here
        inv = lax.rsqrt(dz * dz + dy * dy + dx * dx + smooth_floor)
        return dz * inv, dy * inv, dx * inv

    before = flow(-1)[1][depth:]
    for y in range(rows):
        fz, fy, fx = flow(y)
        fz, fy = fz[depth:], fy[depth:]
        under = jnp.concatenate(spread_row(flow_low, y), axis=0)
        div = fz - jnp.where(level[:flat] == 0, under, pltpu.roll(fz, 1, 0))
        div = div + (fy - before)
        rolled = pltpu.roll(fx, 1, 1)
        div = div + (fx[depth:] - jnp.where(lane[:flat] == 0, rolled[:flat], rolled[depth:]))
        base[y] = own_row(y) + step_size * smooth_weight * div
        before = fy

    total = part_own[...]
    for i in range(chips - 1):
        chip_copy(i).wait_recv()
        total = total + chip_recv[i]
    meas_copy.wait()
    total = total.reshape(tcount, depth, tile)
    for t in range(tcount):
        here = total[t] - meas[0, :, t * tile : (t + 1) * tile]
        res_ref[0, :, t * tile : (t + 1) * tile] = here
        respad[0, margin + t] = here.astype(BF16).astype(F32)
    own_res[...] = respad[0, margin:zero_start].reshape(flat, tile).astype(BF16)

    def same_copy(i):
        return send(own_res, same_recv.at[i], same_ssem.at[i], same_rsem.at[i], slab, 2 * dest[i] + core)

    def forward(i):
        src = own_res if i == chips - 1 else same_recv.at[i]
        return send(src, sibres_recv.at[i], sr_ssem.at[i], sr_rsem.at[i], slab, sib)

    for i in range(chips - 1):
        same_copy(i).start()
    forward(chips - 1).start()

    def back(angle, slot, fresh):
        for y in range(rows):
            pieces = [
                respad[slot, pl.ds(start, tcount)].reshape(flat, tile).astype(BF16)
                for start in starts(angle, y, -1)
            ]
            weights = jnp.concatenate([tiles[angle, y, k] for k in range(band)], axis=1)
            acc = lax.dot_general(
                jnp.concatenate(pieces, axis=1),
                weights,
                (((1,), (1,)), ((), ())),
                preferred_element_type=F32,
            )
            grad[y] = acc if fresh else grad[y] + acc

    def take(block, slot):
        respad[slot, margin:zero_start] = block.astype(F32).reshape(tcount, depth, tile)

    back(me, 0, True)
    forward(chips - 1).wait_recv()
    take(sibres_recv[chips - 1], 1)
    back(sib, 1, False)
    for i in range(chips - 1):
        source = lax.rem(chip + chips - order[i], chips)
        same_copy(i).wait_recv()
        forward(i).start()
        take(same_recv[i], 0)
        back(2 * source + core, 0, False)
        forward(i).wait_recv()
        take(sibres_recv[i], 1)
        back(2 * source + 1 - core, 1, False)

    for y in range(rows):
        out = (base[y] - step_size * grad[y]).reshape(tcount, depth, tile)
        for t in range(tcount):
            upd_ref[:, y, t * tile : (t + 1) * tile] = out[t]

    for there, copy in halos:
        pl.when(there)(copy.wait_send)
    for i in range(chips):
        sib_copy(i).wait_send()
        forward(i).wait_send()
    for i in range(chips - 1):
        chip_copy(i).wait_send()
        same_copy(i).wait_send()


def per_device(slabs, n, volume, measured, ray_tiles, tile_offsets, band_counts):
    depth, rows, width = volume.shape
    count, unused, band, tile, unused_2 = ray_tiles.shape
    tcount = width // tile
    flat = tcount * depth
    padded = 2 * tcount + OFFMAX + band
    chips = n // 2
    dma = pltpu.SemaphoreType.DMA
    vmem = pltpu.VMEM
    block = (flat, tile)
    return pl.pallas_call(
        functools.partial(kernel, slabs, n),
        out_shape=(
            jax.ShapeDtypeStruct(volume.shape, F32),
            jax.ShapeDtypeStruct(measured.shape, F32),
        ),
        in_specs=[pl.BlockSpec(memory_space=pl.ANY)] * 5,
        out_specs=(pl.BlockSpec(memory_space=pltpu.VMEM),) * 2,
        scratch_shapes=[
            vmem(volume.shape, BF16),
            vmem(measured.shape, F32),
            vmem(ray_tiles.shape, BF16),
            vmem(volume.shape, F32),
            vmem((rows, padded, depth, tile), F32),
            vmem(block, F32),
            vmem((chips, *block), F32),
            vmem((chips, *block), F32),
            vmem((chips - 1, *block), F32),
            vmem((chips - 1, *block), F32),
            vmem((chips - 1, *block), BF16),
            vmem((chips, *block), BF16),
            vmem(block, BF16),
            vmem((2, padded, depth, tile), F32),
            vmem((rows, *block), F32),
            vmem((rows, *block), F32),
            vmem((rows, width), F32),
            vmem((2, *block), BF16),
            vmem((2, *block), BF16),
            vmem((2, rows, width), F32),
            vmem((2, rows, width), F32),
            pltpu.SMEM(tile_offsets.shape, jnp.int32),
            pltpu.SMEM(band_counts.shape, jnp.int32),
            dma((4 + n,)),
            dma((chips,)),
            dma((chips,)),
            dma((chips - 1,)),
            dma((chips - 1,)),
            dma((chips - 1,)),
            dma((chips - 1,)),
            dma((chips,)),
            dma((chips,)),
            dma((2,)),
            dma((2,)),
            dma((2,)),
            dma((2,)),
            dma((2,)),
            dma((2,)),
        ],
        compiler_params=pltpu.CompilerParams(
            collective_id=0, has_side_effects=True, vmem_limit_bytes=60 * 1024 * 1024
        ),
        name="step",
    )(volume, measured, ray_tiles, tile_offsets, band_counts)


def solution(mesh):
    return jax.shard_map(
        functools.partial(per_device, mesh.shape["slab"], mesh.shape["angle"]),
        mesh=mesh,
        in_specs=(
            P("slab", "angle", None),
            P("angle", "slab", None),
            P(None, "angle", None, None, None),
            P(),
            P(),
        ),
        out_specs=(P("slab", "angle", None), P("angle", "slab", None)),
        check_vma=False,
    )
```

```python
import functools

import jax
import jax.numpy as jnp
from jax import lax
from jax.experimental import pallas as pl
from jax.experimental.pallas import tpu as pltpu
from jax.sharding import PartitionSpec as P

OFFMAX = 3

step_size = 0.3
smooth_weight = 0.2
smooth_floor = 0.25

F32 = jnp.float32
BF16 = jnp.bfloat16


def kernel(
    slabs,
    n,
    vol_hbm,
    meas_hbm,
    tiles_hbm,
    off_hbm,
    cnt_hbm,
    upd_hbm,
    res_hbm,
    upd_ref,
    res_ref,
    vol_in,
    meas,
    tiles,
    vol32,
    volt,
    part_own,
    sib_send,
    sib_recv,
    chip_send,
    chip_recv,
    same_recv,
    sibres_recv,
    own_res,
    respad,
    grad,
    base,
    flow_low,
    ys,
    yr,
    zr,
    cr,
    off_ref,
    cnt_ref,
    load_sem,
    sib_ssem,
    sib_rsem,
    chip_ssem,
    chip_rsem,
    same_ssem,
    same_rsem,
    sr_ssem,
    sr_rsem,
    y_ssem,
    y_rsem,
    z_ssem,
    z_rsem,
    c_ssem,
    c_rsem,
):
    depth, rows, width = vol_in.shape
    band = tiles.shape[2]
    tile = tiles.shape[3]
    tcount = width // tile
    flat = tcount * depth
    center = band // 2
    margin = OFFMAX + band
    zero_start = margin + tcount
    chips = n // 2

    slab = lax.axis_index("slab")
    me = lax.axis_index("angle")
    chip = lax.div(me, 2)
    core = lax.rem(me, 2)
    sib = me + 1 - 2 * core
    far_y = me - 1 + 2 * core
    first_row = me * rows
    barrier = pltpu.get_barrier_semaphore()

    has_far = (far_y >= 0) & (far_y < n)
    has_zp = slab + 1 < slabs
    has_zm = slab >= 1
    has_yp = me + 1 < n
    has_ym = me >= 1
    has_up = has_zp & has_ym
    has_down = has_zm & has_yp

    def greet(s, a):
        pl.semaphore_signal(barrier, inc=1, device_id=(s, a), device_id_type=pl.DeviceIdType.MESH)

    greet(slab, sib)
    for j in range(1, chips):
        greet(slab, 2 * lax.rem(chip + j, chips) + core)

    pl.when(has_far)(lambda: greet(slab, far_y))
    pl.when(has_zp)(lambda: greet(slab + 1, me))
    pl.when(has_zm)(lambda: greet(slab - 1, me))
    pl.when(has_up)(lambda: greet(slab + 1, me - 1))
    pl.when(has_down)(lambda: greet(slab - 1, me + 1))

    vol_copy = pltpu.make_async_copy(vol_hbm, vol_in, load_sem.at[0])
    vol_copy.start()
    off_copy = pltpu.make_async_copy(off_hbm, off_ref, load_sem.at[n + 2])
    off_copy.start()
    cnt_copy = pltpu.make_async_copy(cnt_hbm, cnt_ref, load_sem.at[n + 3])
    cnt_copy.start()
    order = [chips // 2] + [j for j in range(1, chips) if j != chips // 2] + [0]
    dest = [lax.rem(chip + j, chips) for j in order]
    loads = []
    for i in range(chips):
        pair = []
        for angle, slot in ((2 * dest[i] + 1 - core, 0), (2 * dest[i] + core, 1)):
            copy = pltpu.make_async_copy(
                tiles_hbm.at[angle], tiles.at[angle], load_sem.at[2 + 2 * i + slot]
            )
            copy.start()
            pair.append(copy)
        loads.append(pair)
    meas_copy = pltpu.make_async_copy(meas_hbm, meas, load_sem.at[1])
    meas_copy.start()

    volt[:, :margin] = jnp.zeros((rows, margin, depth, tile), F32)
    volt[:, zero_start:] = jnp.zeros((rows, volt.shape[1] - zero_start, depth, tile), F32)
    respad[:, :margin] = jnp.zeros((2, margin, depth, tile), F32)
    respad[:, zero_start:] = jnp.zeros((2, respad.shape[1] - zero_start, depth, tile), F32)
    vol_copy.wait()
    vol32[...] = vol_in[...].astype(F32)
    for y in range(rows):
        for t in range(tcount):
            volt[y, margin + t] = vol32[:, y, t * tile : (t + 1) * tile]

    def own_row(y):
        return volt[y, margin : margin + tcount].reshape(flat, tile)

    ys[0] = own_row(0).astype(BF16)
    ys[1] = own_row(rows - 1).astype(BF16)

    def send(src, dst, ssem, rsem, s, a):
        return pltpu.make_async_remote_copy(
            src_ref=src,
            dst_ref=dst,
            send_sem=ssem,
            recv_sem=rsem,
            device_id=(s, a),
            device_id_type=pl.DeviceIdType.MESH,
        )

    halos = (
        (has_ym, send(ys.at[0], yr.at[1], y_ssem.at[0], y_rsem.at[1], slab, me - 1)),
        (has_yp, send(ys.at[1], yr.at[0], y_ssem.at[1], y_rsem.at[0], slab, me + 1)),
        (has_zm, send(vol32.at[0], zr.at[1], z_ssem.at[0], z_rsem.at[1], slab - 1, me)),
        (has_zp, send(vol32.at[depth - 1], zr.at[0], z_ssem.at[1], z_rsem.at[0], slab + 1, me)),
        (has_down, send(vol32.at[0], cr.at[1], c_ssem.at[0], c_rsem.at[1], slab - 1, me + 1)),
        (has_up, send(vol32.at[depth - 1], cr.at[0], c_ssem.at[1], c_rsem.at[0], slab + 1, me - 1)),
    )
    arrivals = (
        (has_yp, yr.at[1], send(ys.at[0], yr.at[1], y_ssem.at[0], y_rsem.at[1], slab, me + 1)),
        (has_ym, yr.at[0], send(ys.at[1], yr.at[0], y_ssem.at[1], y_rsem.at[0], slab, me - 1)),
        (has_zp, zr.at[1], send(vol32.at[0], zr.at[1], z_ssem.at[0], z_rsem.at[1], slab + 1, me)),
        (has_zm, zr.at[0], send(vol32.at[depth - 1], zr.at[0], z_ssem.at[1], z_rsem.at[0], slab - 1, me)),
        (has_up, cr.at[1], send(vol32.at[0], cr.at[1], c_ssem.at[0], c_rsem.at[1], slab + 1, me - 1)),
        (has_down, cr.at[0], send(vol32.at[depth - 1], cr.at[0], c_ssem.at[1], c_rsem.at[0], slab - 1, me + 1)),
    )
    def starts(angle, y, sign):
        found = []
        for k in range(band):
            shift = off_ref[angle, first_row + y] + (k - center)
            used = cnt_ref[angle, first_row + y] > k
            found.append(jnp.where(used, margin + sign * shift, zero_start))
        return found

    def view(angle):
        pieces = []
        for y in range(rows):
            for start in starts(angle, y, 1):
                pieces.append(volt[y, pl.ds(start, tcount)].reshape(flat, tile).astype(BF16))
        weights = tiles[angle].reshape(rows * band * tile, tile)
        return jnp.dot(jnp.concatenate(pieces, axis=1), weights, preferred_element_type=F32)

    def sib_copy(i):
        return send(sib_send.at[i], sib_recv.at[i], sib_ssem.at[i], sib_rsem.at[i], slab, sib)

    def chip_copy(i):
        return send(
            chip_send.at[i], chip_recv.at[i], chip_ssem.at[i], chip_rsem.at[i], slab, 2 * dest[i] + core
        )

    def for_sibling(i):
        loads[i][0].wait()
        sib_send[i] = view(2 * dest[i] + 1 - core)

    off_copy.wait()
    cnt_copy.wait()
    for_sibling(0)

    one = jnp.int32(1)
    none = jnp.int32(0)
    expect = jnp.int32(chips)
    for there in (has_far, has_zp, has_zm, has_up, has_down):
        expect = expect + jnp.where(there, one, none)
    pl.semaphore_wait(barrier, expect)

    sib_copy(0).start()
    for there, copy in halos:
        pl.when(there)(copy.start)

    for i in range(chips):
        if i + 1 < chips:
            for_sibling(i + 1)
            sib_copy(i + 1).start()
        loads[i][1].wait()
        part_own[...] = view(2 * dest[i] + core)
        sib_copy(i).wait_recv()
        if i + 1 < chips:
            chip_send[i] = part_own[...] + sib_recv[i]
            chip_copy(i).start()
        else:
            part_own[...] = part_own[...] + sib_recv[i]

    for there, buffer, copy in arrivals:
        pl.when(there)(copy.wait_recv)

        @pl.when(jnp.logical_not(there))
        def _(buffer=buffer):
            buffer[...] = jnp.zeros(buffer.shape, buffer.dtype)

    lane = lax.broadcasted_iota(jnp.int32, (flat + depth, tile), 1)
    level = lax.rem(lax.broadcasted_iota(jnp.int32, (flat + depth, tile), 0), depth)
    zeros_tile = jnp.zeros((depth, tile), F32)

    low = zr[0]
    low_y = jnp.concatenate([low[1:], cr[0][:1]], axis=0)
    low_lane = lax.broadcasted_iota(jnp.int32, (rows, width), 1)
    low_x = jnp.where(low_lane == width - 1, 0.0, pltpu.roll(low, width - 1, 1))
    lz, ly, lx = vol32[0] - low, low_y - low, low_x - low
    flow_low[...] = lz * lax.rsqrt(lz * lz + ly * ly + lx * lx + smooth_floor)

    def field_row(y):
        if 0 <= y < rows:
            return volt[y, margin - 1 : margin + tcount + 1].reshape(flat + 2 * depth, tile)
        inner = yr[0 if y < 0 else 1].astype(F32)
        return jnp.concatenate([zeros_tile, inner, zeros_tile], axis=0)

    def spread_row(ref, row):
        return [
            jnp.broadcast_to(ref[row : row + 1, t * tile : (t + 1) * tile], (depth, tile))
            for t in range(tcount)
        ]

    def flow(y):
        wide = field_row(y)
        here = wide[: flat + depth]
        rolled = pltpu.roll(wide, tile - 1, 1)
        dx = jnp.where(lane == tile - 1, rolled[depth:], rolled[: flat + depth]) - here
        dy = field_row(y + 1)[: flat + depth] - here
        top = spread_row(zr.at[1], y) if y >= 0 else spread_row(cr.at[1], rows - 1)
        top = jnp.concatenate([zeros_tile] + top, axis=0)
        dz = jnp.where(level == depth - 1, top, pltpu.roll(here, flat + depth - 1, 0)) - here
        inv = lax.rsqrt(dz * dz + dy * dy + dx * dx + smooth_floor)
        return dz * inv, dy * inv, dx * inv

    before = flow(-1)[1][depth:]
    for y in range(rows):
        fz, fy, fx = flow(y)
        fz, fy = fz[depth:], fy[depth:]
        under = jnp.concatenate(spread_row(flow_low, y), axis=0)
        div = fz - jnp.where(level[:flat] == 0, under, pltpu.roll(fz, 1, 0))
        div = div + (fy - before)
        rolled = pltpu.roll(fx, 1, 1)
        div = div + (fx[depth:] - jnp.where(lane[:flat] == 0, rolled[:flat], rolled[depth:]))
        base[y] = own_row(y) + step_size * smooth_weight * div
        before = fy

    total = part_own[...]
    for i in range(chips - 1):
        chip_copy(i).wait_recv()
        total = total + chip_recv[i]
    meas_copy.wait()
    total = total.reshape(tcount, depth, tile)
    for t in range(tcount):
        here = total[t] - meas[0, :, t * tile : (t + 1) * tile]
        res_ref[0, :, t * tile : (t + 1) * tile] = here
        respad[0, margin + t] = here.astype(BF16).astype(F32)
    own_res[...] = respad[0, margin:zero_start].reshape(flat, tile).astype(BF16)

    def same_copy(i):
        return send(own_res, same_recv.at[i], same_ssem.at[i], same_rsem.at[i], slab, 2 * dest[i] + core)

    def forward(i):
        src = own_res if i == chips - 1 else same_recv.at[i]
        return send(src, sibres_recv.at[i], sr_ssem.at[i], sr_rsem.at[i], slab, sib)

    for i in range(chips - 1):
        same_copy(i).start()
    forward(chips - 1).start()
    res_copy = pltpu.make_async_copy(res_ref, res_hbm, load_sem.at[n + 4])
    res_copy.start()

    def back(angle, slot, fresh):
        for y in range(rows):
            pieces = [
                respad[slot, pl.ds(start, tcount)].reshape(flat, tile).astype(BF16)
                for start in starts(angle, y, -1)
            ]
            weights = jnp.concatenate([tiles[angle, y, k] for k in range(band)], axis=1)
            acc = lax.dot_general(
                jnp.concatenate(pieces, axis=1),
                weights,
                (((1,), (1,)), ((), ())),
                preferred_element_type=F32,
            )
            grad[y] = acc if fresh else grad[y] + acc

    def take(block, slot):
        respad[slot, margin:zero_start] = block.astype(F32).reshape(tcount, depth, tile)

    back(me, 0, True)
    forward(chips - 1).wait_recv()
    take(sibres_recv[chips - 1], 1)
    back(sib, 1, False)
    for i in range(chips - 1):
        source = lax.rem(chip + chips - order[i], chips)
        same_copy(i).wait_recv()
        forward(i).start()
        take(same_recv[i], 0)
        back(2 * source + core, 0, False)
        forward(i).wait_recv()
        take(sibres_recv[i], 1)
        back(2 * source + 1 - core, 1, False)

    for y in range(rows):
        out = (base[y] - step_size * grad[y]).reshape(tcount, depth, tile)
        for t in range(tcount):
            upd_ref[:, y, t * tile : (t + 1) * tile] = out[t]
    upd_copy = pltpu.make_async_copy(upd_ref, upd_hbm, load_sem.at[n + 5])
    upd_copy.start()

    for there, copy in halos:
        pl.when(there)(copy.wait_send)
    for i in range(chips):
        sib_copy(i).wait_send()
        forward(i).wait_send()
    for i in range(chips - 1):
        chip_copy(i).wait_send()
        same_copy(i).wait_send()
    res_copy.wait()
    upd_copy.wait()


def finish(upd_ref, res_ref, upd_out, res_out, sem):
    copies = (
        pltpu.make_async_copy(upd_ref, upd_out, sem.at[0]),
        pltpu.make_async_copy(res_ref, res_out, sem.at[1]),
    )
    for copy in copies:
        copy.start()
    for copy in copies:
        copy.wait()


def per_device(slabs, n, volume, measured, ray_tiles, tile_offsets, band_counts):
    depth, rows, width = volume.shape
    count, unused, band, tile, unused_2 = ray_tiles.shape
    tcount = width // tile
    flat = tcount * depth
    padded = 2 * tcount + OFFMAX + band
    chips = n // 2
    dma = pltpu.SemaphoreType.DMA
    vmem = pltpu.VMEM
    block = (flat, tile)
    shapes = (
        jax.ShapeDtypeStruct(volume.shape, F32),
        jax.ShapeDtypeStruct(measured.shape, F32),
    )
    updated, residual = pl.pallas_call(
        functools.partial(kernel, slabs, n),
        out_shape=shapes,
        in_specs=[pl.BlockSpec(memory_space=pl.ANY)] * 5,
        out_specs=(pl.BlockSpec(memory_space=pl.ANY),) * 2,
        scratch_shapes=[
            vmem(volume.shape, F32),
            vmem(measured.shape, F32),
            vmem(volume.shape, BF16),
            vmem(measured.shape, F32),
            vmem(ray_tiles.shape, BF16),
            vmem(volume.shape, F32),
            vmem((rows, padded, depth, tile), F32),
            vmem(block, F32),
            vmem((chips, *block), F32),
            vmem((chips, *block), F32),
            vmem((chips - 1, *block), F32),
            vmem((chips - 1, *block), F32),
            vmem((chips - 1, *block), BF16),
            vmem((chips, *block), BF16),
            vmem(block, BF16),
            vmem((2, padded, depth, tile), F32),
            vmem((rows, *block), F32),
            vmem((rows, *block), F32),
            vmem((rows, width), F32),
            vmem((2, *block), BF16),
            vmem((2, *block), BF16),
            vmem((2, rows, width), F32),
            vmem((2, rows, width), F32),
            pltpu.SMEM(tile_offsets.shape, jnp.int32),
            pltpu.SMEM(band_counts.shape, jnp.int32),
            dma((6 + n,)),
            dma((chips,)),
            dma((chips,)),
            dma((chips - 1,)),
            dma((chips - 1,)),
            dma((chips - 1,)),
            dma((chips - 1,)),
            dma((chips,)),
            dma((chips,)),
            dma((2,)),
            dma((2,)),
            dma((2,)),
            dma((2,)),
            dma((2,)),
            dma((2,)),
        ],
        compiler_params=pltpu.CompilerParams(
            collective_id=0, has_side_effects=True, vmem_limit_bytes=60 * 1024 * 1024
        ),
        name="step",
    )(volume, measured, ray_tiles, tile_offsets, band_counts)
    return pl.pallas_call(
        finish,
        out_shape=shapes,
        in_specs=[pl.BlockSpec(memory_space=pl.ANY)] * 2,
        out_specs=(pl.BlockSpec(memory_space=pl.ANY),) * 2,
        scratch_shapes=[dma((2,))],
        compiler_params=pltpu.CompilerParams(vmem_limit_bytes=60 * 1024 * 1024),
        name="finish",
    )(updated, residual)


def solution(mesh):
    return jax.shard_map(
        functools.partial(per_device, mesh.shape["slab"], mesh.shape["angle"]),
        mesh=mesh,
        in_specs=(
            P("slab", "angle", None),
            P("angle", "slab", None),
            P(None, "angle", None, None, None),
            P(),
            P(),
        ),
        out_specs=(P("slab", "angle", None), P("angle", "slab", None)),
        check_vma=False,
    )
```

```python
import functools

import jax
import jax.numpy as jnp
from jax import lax
from jax.experimental import pallas as pl
from jax.experimental.pallas import tpu as pltpu
from jax.sharding import PartitionSpec as P

OFFMAX = 3

step_size = 0.3
smooth_weight = 0.2
smooth_floor = 0.25

F32 = jnp.float32
BF16 = jnp.bfloat16


def kernel(
    slabs,
    n,
    vol_hbm,
    meas_hbm,
    tiles_hbm,
    off_hbm,
    cnt_hbm,
    upd_hbm,
    res_hbm,
    upd_ref,
    res_ref,
    vol_in,
    meas,
    tiles,
    vol32,
    volt,
    part_own,
    sib_send,
    sib_recv,
    chip_send,
    chip_recv,
    relay_recv,
    same_recv,
    sibres_recv,
    own_res,
    respad,
    grad,
    base,
    flow_low,
    ys,
    yr,
    zr,
    cr,
    off_ref,
    cnt_ref,
    load_sem,
    sib_ssem,
    sib_rsem,
    chip_ssem,
    chip_rsem,
    relay_rsem,
    same_ssem,
    same_rsem,
    sr_ssem,
    sr_rsem,
    y_ssem,
    y_rsem,
    z_ssem,
    z_rsem,
    c_ssem,
    c_rsem,
):
    depth, rows, width = vol_in.shape
    band = tiles.shape[2]
    tile = tiles.shape[3]
    tcount = width // tile
    flat = tcount * depth
    center = band // 2
    margin = OFFMAX + band
    zero_start = margin + tcount
    chips = n // 2

    slab = lax.axis_index("slab")
    me = lax.axis_index("angle")
    chip = lax.div(me, 2)
    core = lax.rem(me, 2)
    sib = me + 1 - 2 * core
    far_y = me - 1 + 2 * core
    first_row = me * rows
    barrier = pltpu.get_barrier_semaphore()

    has_far = (far_y >= 0) & (far_y < n)
    has_zp = slab + 1 < slabs
    has_zm = slab >= 1
    has_yp = me + 1 < n
    has_ym = me >= 1
    has_up = has_zp & has_ym
    has_down = has_zm & has_yp

    def greet(s, a):
        pl.semaphore_signal(barrier, inc=1, device_id=(s, a), device_id_type=pl.DeviceIdType.MESH)

    greet(slab, sib)
    for j in range(1, chips):
        greet(slab, 2 * lax.rem(chip + j, chips) + core)

    pl.when(has_far)(lambda: greet(slab, far_y))
    pl.when(has_zp)(lambda: greet(slab + 1, me))
    pl.when(has_zm)(lambda: greet(slab - 1, me))
    pl.when(has_up)(lambda: greet(slab + 1, me - 1))
    pl.when(has_down)(lambda: greet(slab - 1, me + 1))

    vol_copy = pltpu.make_async_copy(vol_hbm, vol_in, load_sem.at[0])
    vol_copy.start()
    off_copy = pltpu.make_async_copy(off_hbm, off_ref, load_sem.at[n + 2])
    off_copy.start()
    cnt_copy = pltpu.make_async_copy(cnt_hbm, cnt_ref, load_sem.at[n + 3])
    cnt_copy.start()
    order = [chips // 2] + [j for j in range(1, chips) if j != chips // 2] + [0]
    peer = [lax.rem(chip + j, chips) for j in order]
    relayed = chips == 4
    half = lax.div(chip, 2)
    mate = chip + 1 - 2 * lax.rem(chip, 2)
    middle = (chip >= 1) & (chip < chips - 1)
    if relayed:
        dest = [3 - 3 * half, 2 - half, mate, chip]
    else:
        dest = peer
    loads = []
    for i in range(chips):
        pair = []
        for angle, slot in ((2 * dest[i] + 1 - core, 0), (2 * dest[i] + core, 1)):
            copy = pltpu.make_async_copy(
                tiles_hbm.at[angle], tiles.at[angle], load_sem.at[2 + 2 * i + slot]
            )
            copy.start()
            pair.append(copy)
        loads.append(pair)
    meas_copy = pltpu.make_async_copy(meas_hbm, meas, load_sem.at[1])
    meas_copy.start()

    volt[:, :margin] = jnp.zeros((rows, margin, depth, tile), F32)
    volt[:, zero_start:] = jnp.zeros((rows, volt.shape[1] - zero_start, depth, tile), F32)
    respad[:, :margin] = jnp.zeros((2, margin, depth, tile), F32)
    respad[:, zero_start:] = jnp.zeros((2, respad.shape[1] - zero_start, depth, tile), F32)
    vol_copy.wait()
    vol32[...] = vol_in[...].astype(F32)
    for y in range(rows):
        for t in range(tcount):
            volt[y, margin + t] = vol32[:, y, t * tile : (t + 1) * tile]

    def own_row(y):
        return volt[y, margin : margin + tcount].reshape(flat, tile)

    ys[0] = own_row(0).astype(BF16)
    ys[1] = own_row(rows - 1).astype(BF16)

    def send(src, dst, ssem, rsem, s, a):
        return pltpu.make_async_remote_copy(
            src_ref=src,
            dst_ref=dst,
            send_sem=ssem,
            recv_sem=rsem,
            device_id=(s, a),
            device_id_type=pl.DeviceIdType.MESH,
        )

    halos = (
        (has_ym, send(ys.at[0], yr.at[1], y_ssem.at[0], y_rsem.at[1], slab, me - 1)),
        (has_yp, send(ys.at[1], yr.at[0], y_ssem.at[1], y_rsem.at[0], slab, me + 1)),
        (has_zm, send(vol32.at[0], zr.at[1], z_ssem.at[0], z_rsem.at[1], slab - 1, me)),
        (has_zp, send(vol32.at[depth - 1], zr.at[0], z_ssem.at[1], z_rsem.at[0], slab + 1, me)),
        (has_down, send(vol32.at[0], cr.at[1], c_ssem.at[0], c_rsem.at[1], slab - 1, me + 1)),
        (has_up, send(vol32.at[depth - 1], cr.at[0], c_ssem.at[1], c_rsem.at[0], slab + 1, me - 1)),
    )
    arrivals = (
        (has_yp, yr.at[1], send(ys.at[0], yr.at[1], y_ssem.at[0], y_rsem.at[1], slab, me + 1)),
        (has_ym, yr.at[0], send(ys.at[1], yr.at[0], y_ssem.at[1], y_rsem.at[0], slab, me - 1)),
        (has_zp, zr.at[1], send(vol32.at[0], zr.at[1], z_ssem.at[0], z_rsem.at[1], slab + 1, me)),
        (has_zm, zr.at[0], send(vol32.at[depth - 1], zr.at[0], z_ssem.at[1], z_rsem.at[0], slab - 1, me)),
        (has_up, cr.at[1], send(vol32.at[0], cr.at[1], c_ssem.at[0], c_rsem.at[1], slab + 1, me - 1)),
        (has_down, cr.at[0], send(vol32.at[depth - 1], cr.at[0], c_ssem.at[1], c_rsem.at[0], slab - 1, me + 1)),
    )
    def starts(angle, y, sign):
        found = []
        for k in range(band):
            shift = off_ref[angle, first_row + y] + (k - center)
            used = cnt_ref[angle, first_row + y] > k
            found.append(jnp.where(used, margin + sign * shift, zero_start))
        return found

    def view(angle):
        pieces = []
        for y in range(rows):
            for start in starts(angle, y, 1):
                pieces.append(volt[y, pl.ds(start, tcount)].reshape(flat, tile).astype(BF16))
        weights = tiles[angle].reshape(rows * band * tile, tile)
        return jnp.dot(jnp.concatenate(pieces, axis=1), weights, preferred_element_type=F32)

    def sib_copy(i):
        return send(sib_send.at[i], sib_recv.at[i], sib_ssem.at[i], sib_rsem.at[i], slab, sib)

    def chip_copy(i):
        return send(
            chip_send.at[i], chip_recv.at[i], chip_ssem.at[i], chip_rsem.at[i], slab, 2 * dest[i] + core
        )

    def for_sibling(i):
        loads[i][0].wait()
        sib_send[i] = view(2 * dest[i] + 1 - core)

    off_copy.wait()
    cnt_copy.wait()
    def relay_copy(i):
        return send(
            chip_send.at[i], relay_recv.at[i], chip_ssem.at[i], relay_rsem.at[i], slab, 2 * mate + core
        )

    def far_copy(i):
        return send(
            chip_send.at[i], chip_recv.at[0], chip_ssem.at[i], chip_rsem.at[0], slab, 2 * dest[i] + core
        )

    def near_copy():
        return send(
            chip_send.at[2], chip_recv.at[1], chip_ssem.at[2], chip_rsem.at[1], slab, 2 * mate + core
        )

    for_sibling(0)

    one = jnp.int32(1)
    none = jnp.int32(0)
    expect = jnp.int32(chips)
    for there in (has_far, has_zp, has_zm, has_up, has_down):
        expect = expect + jnp.where(there, one, none)
    pl.semaphore_wait(barrier, expect)

    sib_copy(0).start()
    for there, copy in halos:
        pl.when(there)(copy.start)

    for i in range(chips):
        if i + 1 < chips:
            for_sibling(i + 1)
            sib_copy(i + 1).start()
        loads[i][1].wait()
        part_own[...] = view(2 * dest[i] + core)
        sib_copy(i).wait_recv()
        if i + 1 < chips:
            chip_send[i] = part_own[...] + sib_recv[i]
            if not relayed:
                chip_copy(i).start()
            elif i < 2:
                pl.when(jnp.logical_not(middle))(relay_copy(i).start)
            else:
                near_copy().start()
        else:
            part_own[...] = part_own[...] + sib_recv[i]

    if relayed:

        @pl.when(middle)
        def _():
            for i in range(2):
                relay_copy(i).wait_recv()
                chip_send[i] = chip_send[i] + relay_recv[i]
                far_copy(i).start()

    for there, buffer, copy in arrivals:
        pl.when(there)(copy.wait_recv)

        @pl.when(jnp.logical_not(there))
        def _(buffer=buffer):
            buffer[...] = jnp.zeros(buffer.shape, buffer.dtype)

    lane = lax.broadcasted_iota(jnp.int32, (flat + depth, tile), 1)
    level = lax.rem(lax.broadcasted_iota(jnp.int32, (flat + depth, tile), 0), depth)
    zeros_tile = jnp.zeros((depth, tile), F32)

    low = zr[0]
    low_y = jnp.concatenate([low[1:], cr[0][:1]], axis=0)
    low_lane = lax.broadcasted_iota(jnp.int32, (rows, width), 1)
    low_x = jnp.where(low_lane == width - 1, 0.0, pltpu.roll(low, width - 1, 1))
    lz, ly, lx = vol32[0] - low, low_y - low, low_x - low
    flow_low[...] = lz * lax.rsqrt(lz * lz + ly * ly + lx * lx + smooth_floor)

    def field_row(y):
        if 0 <= y < rows:
            return volt[y, margin - 1 : margin + tcount + 1].reshape(flat + 2 * depth, tile)
        inner = yr[0 if y < 0 else 1].astype(F32)
        return jnp.concatenate([zeros_tile, inner, zeros_tile], axis=0)

    def spread_row(ref, row):
        return [
            jnp.broadcast_to(ref[row : row + 1, t * tile : (t + 1) * tile], (depth, tile))
            for t in range(tcount)
        ]

    def flow(y):
        wide = field_row(y)
        here = wide[: flat + depth]
        rolled = pltpu.roll(wide, tile - 1, 1)
        dx = jnp.where(lane == tile - 1, rolled[depth:], rolled[: flat + depth]) - here
        dy = field_row(y + 1)[: flat + depth] - here
        top = spread_row(zr.at[1], y) if y >= 0 else spread_row(cr.at[1], rows - 1)
        top = jnp.concatenate([zeros_tile] + top, axis=0)
        dz = jnp.where(level == depth - 1, top, pltpu.roll(here, flat + depth - 1, 0)) - here
        inv = lax.rsqrt(dz * dz + dy * dy + dx * dx + smooth_floor)
        return dz * inv, dy * inv, dx * inv

    before = flow(-1)[1][depth:]
    for y in range(rows):
        fz, fy, fx = flow(y)
        fz, fy = fz[depth:], fy[depth:]
        under = jnp.concatenate(spread_row(flow_low, y), axis=0)
        div = fz - jnp.where(level[:flat] == 0, under, pltpu.roll(fz, 1, 0))
        div = div + (fy - before)
        rolled = pltpu.roll(fx, 1, 1)
        div = div + (fx[depth:] - jnp.where(lane[:flat] == 0, rolled[:flat], rolled[depth:]))
        base[y] = own_row(y) + step_size * smooth_weight * div
        before = fy

    total = part_own[...]
    if relayed:
        near_copy().wait_recv()
        total = total + chip_recv[1]
        far_copy(0).wait_recv()
        total = total + chip_recv[0]
    else:
        for i in range(chips - 1):
            chip_copy(i).wait_recv()
            total = total + chip_recv[i]
    meas_copy.wait()
    total = total.reshape(tcount, depth, tile)
    for t in range(tcount):
        here = total[t] - meas[0, :, t * tile : (t + 1) * tile]
        res_ref[0, :, t * tile : (t + 1) * tile] = here
        respad[0, margin + t] = here.astype(BF16).astype(F32)
    own_res[...] = respad[0, margin:zero_start].reshape(flat, tile).astype(BF16)

    def same_copy(i):
        return send(own_res, same_recv.at[i], same_ssem.at[i], same_rsem.at[i], slab, 2 * peer[i] + core)

    def forward(i):
        src = own_res if i == chips - 1 else same_recv.at[i]
        return send(src, sibres_recv.at[i], sr_ssem.at[i], sr_rsem.at[i], slab, sib)

    for i in range(chips - 1):
        same_copy(i).start()
    forward(chips - 1).start()
    res_copy = pltpu.make_async_copy(res_ref, res_hbm, load_sem.at[n + 4])
    res_copy.start()

    def back(angle, slot, fresh):
        for y in range(rows):
            pieces = [
                respad[slot, pl.ds(start, tcount)].reshape(flat, tile).astype(BF16)
                for start in starts(angle, y, -1)
            ]
            weights = jnp.concatenate([tiles[angle, y, k] for k in range(band)], axis=1)
            acc = lax.dot_general(
                jnp.concatenate(pieces, axis=1),
                weights,
                (((1,), (1,)), ((), ())),
                preferred_element_type=F32,
            )
            grad[y] = acc if fresh else grad[y] + acc

    def take(block, slot):
        respad[slot, margin:zero_start] = block.astype(F32).reshape(tcount, depth, tile)

    back(me, 0, True)
    forward(chips - 1).wait_recv()
    take(sibres_recv[chips - 1], 1)
    back(sib, 1, False)
    for i in range(chips - 1):
        source = lax.rem(chip + chips - order[i], chips)
        same_copy(i).wait_recv()
        forward(i).start()
        take(same_recv[i], 0)
        back(2 * source + core, 0, False)
        forward(i).wait_recv()
        take(sibres_recv[i], 1)
        back(2 * source + 1 - core, 1, False)

    for y in range(rows):
        out = (base[y] - step_size * grad[y]).reshape(tcount, depth, tile)
        for t in range(tcount):
            upd_ref[:, y, t * tile : (t + 1) * tile] = out[t]
    upd_copy = pltpu.make_async_copy(upd_ref, upd_hbm, load_sem.at[n + 5])
    upd_copy.start()

    for there, copy in halos:
        pl.when(there)(copy.wait_send)
    for i in range(chips):
        sib_copy(i).wait_send()
        forward(i).wait_send()
    for i in range(chips - 1):
        chip_copy(i).wait_send()
        same_copy(i).wait_send()
    res_copy.wait()
    upd_copy.wait()


def finish(upd_in, res_in, upd_out, res_out, upd, res, sem):
    parts = sem.shape[1] - 1
    size = upd.shape[0] // parts
    pairs = [(res_in, res, res_out)]
    for i in range(parts):
        span = pl.ds(i * size, size)
        pairs.append((upd_in.at[span], upd.at[span], upd_out.at[span]))
    reads = [pltpu.make_async_copy(p[0], p[1], sem.at[0, i]) for i, p in enumerate(pairs)]
    writes = [pltpu.make_async_copy(p[1], p[2], sem.at[1, i]) for i, p in enumerate(pairs)]
    for read in reads:
        read.start()
    for read, write in zip(reads, writes):
        read.wait()
        write.start()
    for write in writes:
        write.wait()


def per_device(slabs, n, volume, measured, ray_tiles, tile_offsets, band_counts):
    depth, rows, width = volume.shape
    count, unused, band, tile, unused_2 = ray_tiles.shape
    tcount = width // tile
    flat = tcount * depth
    padded = 2 * tcount + OFFMAX + band
    chips = n // 2
    dma = pltpu.SemaphoreType.DMA
    vmem = pltpu.VMEM
    block = (flat, tile)
    shapes = (
        jax.ShapeDtypeStruct(volume.shape, F32),
        jax.ShapeDtypeStruct(measured.shape, F32),
    )
    updated, residual = pl.pallas_call(
        functools.partial(kernel, slabs, n),
        out_shape=shapes,
        in_specs=[pl.BlockSpec(memory_space=pl.ANY)] * 5,
        out_specs=(pl.BlockSpec(memory_space=pl.ANY),) * 2,
        scratch_shapes=[
            vmem(volume.shape, F32),
            vmem(measured.shape, F32),
            vmem(volume.shape, BF16),
            vmem(measured.shape, F32),
            vmem(ray_tiles.shape, BF16),
            vmem(volume.shape, F32),
            vmem((rows, padded, depth, tile), F32),
            vmem(block, F32),
            vmem((chips, *block), F32),
            vmem((chips, *block), F32),
            vmem((chips - 1, *block), F32),
            vmem((chips - 1, *block), F32),
            vmem((2, *block), F32),
            vmem((chips - 1, *block), BF16),
            vmem((chips, *block), BF16),
            vmem(block, BF16),
            vmem((2, padded, depth, tile), F32),
            vmem((rows, *block), F32),
            vmem((rows, *block), F32),
            vmem((rows, width), F32),
            vmem((2, *block), BF16),
            vmem((2, *block), BF16),
            vmem((2, rows, width), F32),
            vmem((2, rows, width), F32),
            pltpu.SMEM(tile_offsets.shape, jnp.int32),
            pltpu.SMEM(band_counts.shape, jnp.int32),
            dma((6 + n,)),
            dma((chips,)),
            dma((chips,)),
            dma((chips - 1,)),
            dma((chips - 1,)),
            dma((2,)),
            dma((chips - 1,)),
            dma((chips - 1,)),
            dma((chips,)),
            dma((chips,)),
            dma((2,)),
            dma((2,)),
            dma((2,)),
            dma((2,)),
            dma((2,)),
            dma((2,)),
        ],
        compiler_params=pltpu.CompilerParams(
            collective_id=0, has_side_effects=True, vmem_limit_bytes=60 * 1024 * 1024
        ),
        name="step",
    )(volume, measured, ray_tiles, tile_offsets, band_counts)
    return pl.pallas_call(
        finish,
        out_shape=shapes,
        in_specs=[pl.BlockSpec(memory_space=pl.ANY)] * 2,
        out_specs=(pl.BlockSpec(memory_space=pl.ANY),) * 2,
        scratch_shapes=[vmem(volume.shape, F32), vmem(measured.shape, F32), dma((2, 5))],
        compiler_params=pltpu.CompilerParams(vmem_limit_bytes=60 * 1024 * 1024),
        name="finish",
    )(updated, residual)


def solution(mesh):
    return jax.shard_map(
        functools.partial(per_device, mesh.shape["slab"], mesh.shape["angle"]),
        mesh=mesh,
        in_specs=(
            P("slab", "angle", None),
            P("angle", "slab", None),
            P(None, "angle", None, None, None),
            P(),
            P(),
        ),
        out_specs=(P("slab", "angle", None), P("angle", "slab", None)),
        check_vma=False,
    )
```

```python
import functools

import jax
import jax.numpy as jnp
from jax import lax
from jax.experimental import pallas as pl
from jax.experimental.pallas import tpu as pltpu
from jax.sharding import PartitionSpec as P

OFFMAX = 3

step_size = 0.3
smooth_weight = 0.2
smooth_floor = 0.25

F32 = jnp.float32
BF16 = jnp.bfloat16


def kernel(
    slabs,
    n,
    vol_hbm,
    meas_hbm,
    tiles_hbm,
    off_hbm,
    cnt_hbm,
    upd_hbm,
    res_hbm,
    upd_ref,
    res_ref,
    vol_in,
    meas,
    tiles,
    turned,
    vol32,
    volt,
    part_own,
    sib_send,
    sib_recv,
    chip_send,
    chip_recv,
    same_recv,
    sibres_recv,
    own_res,
    respad,
    grad,
    base,
    flow_low,
    ys,
    yr,
    zr,
    cr,
    off_ref,
    cnt_ref,
    load_sem,
    sib_ssem,
    sib_rsem,
    chip_ssem,
    chip_rsem,
    same_ssem,
    same_rsem,
    sr_ssem,
    sr_rsem,
    y_ssem,
    y_rsem,
    z_ssem,
    z_rsem,
    c_ssem,
    c_rsem,
):
    depth, rows, width = vol_in.shape
    band = tiles.shape[2]
    tile = tiles.shape[3]
    tcount = width // tile
    flat = tcount * depth
    center = band // 2
    margin = OFFMAX + band
    zero_start = margin + tcount
    chips = n // 2

    slab = lax.axis_index("slab")
    me = lax.axis_index("angle")
    chip = lax.div(me, 2)
    core = lax.rem(me, 2)
    sib = me + 1 - 2 * core
    far_y = me - 1 + 2 * core
    first_row = me * rows
    barrier = pltpu.get_barrier_semaphore()

    has_far = (far_y >= 0) & (far_y < n)
    has_zp = slab + 1 < slabs
    has_zm = slab >= 1
    has_yp = me + 1 < n
    has_ym = me >= 1
    has_up = has_zp & has_ym
    has_down = has_zm & has_yp

    def greet(s, a):
        pl.semaphore_signal(barrier, inc=1, device_id=(s, a), device_id_type=pl.DeviceIdType.MESH)

    greet(slab, sib)
    for j in range(1, chips):
        greet(slab, 2 * lax.rem(chip + j, chips) + core)

    pl.when(has_far)(lambda: greet(slab, far_y))
    pl.when(has_zp)(lambda: greet(slab + 1, me))
    pl.when(has_zm)(lambda: greet(slab - 1, me))
    pl.when(has_up)(lambda: greet(slab + 1, me - 1))
    pl.when(has_down)(lambda: greet(slab - 1, me + 1))

    vol_copy = pltpu.make_async_copy(vol_hbm, vol_in, load_sem.at[0])
    vol_copy.start()
    off_copy = pltpu.make_async_copy(off_hbm, off_ref, load_sem.at[n + 2])
    off_copy.start()
    cnt_copy = pltpu.make_async_copy(cnt_hbm, cnt_ref, load_sem.at[n + 3])
    cnt_copy.start()
    order = [chips // 2] + [j for j in range(1, chips) if j != chips // 2] + [0]
    dest = [lax.rem(chip + j, chips) for j in order]
    loads = []
    for i in range(chips):
        pair = []
        for angle, slot in ((2 * dest[i] + 1 - core, 0), (2 * dest[i] + core, 1)):
            copy = pltpu.make_async_copy(
                tiles_hbm.at[angle], tiles.at[angle], load_sem.at[2 + 2 * i + slot]
            )
            copy.start()
            pair.append(copy)
        loads.append(pair)
    meas_copy = pltpu.make_async_copy(meas_hbm, meas, load_sem.at[1])
    meas_copy.start()

    volt[:, :margin] = jnp.zeros((rows, margin, depth, tile), F32)
    volt[:, zero_start:] = jnp.zeros((rows, volt.shape[1] - zero_start, depth, tile), F32)
    respad[:, :margin] = jnp.zeros((2, margin, depth, tile), F32)
    respad[:, zero_start:] = jnp.zeros((2, respad.shape[1] - zero_start, depth, tile), F32)
    vol_copy.wait()
    vol32[...] = vol_in[...].astype(F32)
    for y in range(rows):
        for t in range(tcount):
            volt[y, margin + t] = vol32[:, y, t * tile : (t + 1) * tile]

    def own_row(y):
        return volt[y, margin : margin + tcount].reshape(flat, tile)

    ys[0] = own_row(0).astype(BF16)
    ys[1] = own_row(rows - 1).astype(BF16)

    def send(src, dst, ssem, rsem, s, a):
        return pltpu.make_async_remote_copy(
            src_ref=src,
            dst_ref=dst,
            send_sem=ssem,
            recv_sem=rsem,
            device_id=(s, a),
            device_id_type=pl.DeviceIdType.MESH,
        )

    halos = (
        (has_ym, send(ys.at[0], yr.at[1], y_ssem.at[0], y_rsem.at[1], slab, me - 1)),
        (has_yp, send(ys.at[1], yr.at[0], y_ssem.at[1], y_rsem.at[0], slab, me + 1)),
        (has_zm, send(vol32.at[0], zr.at[1], z_ssem.at[0], z_rsem.at[1], slab - 1, me)),
        (has_zp, send(vol32.at[depth - 1], zr.at[0], z_ssem.at[1], z_rsem.at[0], slab + 1, me)),
        (has_down, send(vol32.at[0], cr.at[1], c_ssem.at[0], c_rsem.at[1], slab - 1, me + 1)),
        (has_up, send(vol32.at[depth - 1], cr.at[0], c_ssem.at[1], c_rsem.at[0], slab + 1, me - 1)),
    )
    arrivals = (
        (has_yp, yr.at[1], send(ys.at[0], yr.at[1], y_ssem.at[0], y_rsem.at[1], slab, me + 1)),
        (has_ym, yr.at[0], send(ys.at[1], yr.at[0], y_ssem.at[1], y_rsem.at[0], slab, me - 1)),
        (has_zp, zr.at[1], send(vol32.at[0], zr.at[1], z_ssem.at[0], z_rsem.at[1], slab + 1, me)),
        (has_zm, zr.at[0], send(vol32.at[depth - 1], zr.at[0], z_ssem.at[1], z_rsem.at[0], slab - 1, me)),
        (has_up, cr.at[1], send(vol32.at[0], cr.at[1], c_ssem.at[0], c_rsem.at[1], slab + 1, me - 1)),
        (has_down, cr.at[0], send(vol32.at[depth - 1], cr.at[0], c_ssem.at[1], c_rsem.at[0], slab - 1, me + 1)),
    )
    def starts(angle, y, sign):
        found = []
        for k in range(band):
            shift = off_ref[angle, first_row + y] + (k - center)
            used = cnt_ref[angle, first_row + y] > k
            found.append(jnp.where(used, margin + sign * shift, zero_start))
        return found

    def view(angle):
        pieces = []
        for y in range(rows):
            for start in starts(angle, y, 1):
                pieces.append(volt[y, pl.ds(start, tcount)].reshape(flat, tile).astype(BF16))
        weights = tiles[angle].reshape(rows * band * tile, tile)
        return jnp.dot(jnp.concatenate(pieces, axis=1), weights, preferred_element_type=F32)

    def sib_copy(i):
        return send(sib_send.at[i], sib_recv.at[i], sib_ssem.at[i], sib_rsem.at[i], slab, sib)

    def chip_copy(i):
        return send(
            chip_send.at[i], chip_recv.at[i], chip_ssem.at[i], chip_rsem.at[i], slab, 2 * dest[i] + core
        )

    def for_sibling(i):
        loads[i][0].wait()
        sib_send[i] = view(2 * dest[i] + 1 - core)

    off_copy.wait()
    cnt_copy.wait()
    for_sibling(0)

    one = jnp.int32(1)
    none = jnp.int32(0)
    expect = jnp.int32(chips)
    for there in (has_far, has_zp, has_zm, has_up, has_down):
        expect = expect + jnp.where(there, one, none)
    pl.semaphore_wait(barrier, expect)

    sib_copy(0).start()
    for there, copy in halos:
        pl.when(there)(copy.start)

    for i in range(chips):
        if i + 1 < chips:
            for_sibling(i + 1)
            sib_copy(i + 1).start()
        loads[i][1].wait()
        part_own[...] = view(2 * dest[i] + core)
        sib_copy(i).wait_recv()
        if i + 1 < chips:
            chip_send[i] = part_own[...] + sib_recv[i]
            chip_copy(i).start()
        else:
            part_own[...] = part_own[...] + sib_recv[i]

    @pl.loop(0, n)
    def _(angle):
        for y in range(rows):
            for k in range(band):
                turned[angle, y, k * tile : (k + 1) * tile] = tiles[angle, y, k].T

    for there, buffer, copy in arrivals:
        pl.when(there)(copy.wait_recv)

        @pl.when(jnp.logical_not(there))
        def _(buffer=buffer):
            buffer[...] = jnp.zeros(buffer.shape, buffer.dtype)

    lane = lax.broadcasted_iota(jnp.int32, (flat + depth, tile), 1)
    level = lax.rem(lax.broadcasted_iota(jnp.int32, (flat + depth, tile), 0), depth)
    zeros_tile = jnp.zeros((depth, tile), F32)

    low = zr[0]
    low_y = jnp.concatenate([low[1:], cr[0][:1]], axis=0)
    low_lane = lax.broadcasted_iota(jnp.int32, (rows, width), 1)
    low_x = jnp.where(low_lane == width - 1, 0.0, pltpu.roll(low, width - 1, 1))
    lz, ly, lx = vol32[0] - low, low_y - low, low_x - low
    flow_low[...] = lz * lax.rsqrt(lz * lz + ly * ly + lx * lx + smooth_floor)

    def field_row(y):
        if 0 <= y < rows:
            return volt[y, margin - 1 : margin + tcount + 1].reshape(flat + 2 * depth, tile)
        inner = yr[0 if y < 0 else 1].astype(F32)
        return jnp.concatenate([zeros_tile, inner, zeros_tile], axis=0)

    def spread_row(ref, row):
        return [
            jnp.broadcast_to(ref[row : row + 1, t * tile : (t + 1) * tile], (depth, tile))
            for t in range(tcount)
        ]

    def flow(y):
        wide = field_row(y)
        here = wide[: flat + depth]
        rolled = pltpu.roll(wide, tile - 1, 1)
        dx = jnp.where(lane == tile - 1, rolled[depth:], rolled[: flat + depth]) - here
        dy = field_row(y + 1)[: flat + depth] - here
        top = spread_row(zr.at[1], y) if y >= 0 else spread_row(cr.at[1], rows - 1)
        top = jnp.concatenate([zeros_tile] + top, axis=0)
        dz = jnp.where(level == depth - 1, top, pltpu.roll(here, flat + depth - 1, 0)) - here
        inv = lax.rsqrt(dz * dz + dy * dy + dx * dx + smooth_floor)
        return dz * inv, dy * inv, dx * inv

    before = flow(-1)[1][depth:]
    for y in range(rows):
        fz, fy, fx = flow(y)
        fz, fy = fz[depth:], fy[depth:]
        under = jnp.concatenate(spread_row(flow_low, y), axis=0)
        div = fz - jnp.where(level[:flat] == 0, under, pltpu.roll(fz, 1, 0))
        div = div + (fy - before)
        rolled = pltpu.roll(fx, 1, 1)
        div = div + (fx[depth:] - jnp.where(lane[:flat] == 0, rolled[:flat], rolled[depth:]))
        base[y] = own_row(y) + step_size * smooth_weight * div
        before = fy

    total = part_own[...]
    for i in range(chips - 1):
        chip_copy(i).wait_recv()
        total = total + chip_recv[i]
    meas_copy.wait()
    total = total.reshape(tcount, depth, tile)
    for t in range(tcount):
        here = total[t] - meas[0, :, t * tile : (t + 1) * tile]
        res_ref[0, :, t * tile : (t + 1) * tile] = here
        respad[0, margin + t] = here.astype(BF16).astype(F32)
    own_res[...] = respad[0, margin:zero_start].reshape(flat, tile).astype(BF16)

    def same_copy(i):
        return send(own_res, same_recv.at[i], same_ssem.at[i], same_rsem.at[i], slab, 2 * dest[i] + core)

    def forward(i):
        src = own_res if i == chips - 1 else same_recv.at[i]
        return send(src, sibres_recv.at[i], sr_ssem.at[i], sr_rsem.at[i], slab, sib)

    for i in range(chips - 1):
        same_copy(i).start()
    forward(chips - 1).start()
    res_copy = pltpu.make_async_copy(res_ref, res_hbm, load_sem.at[n + 4])
    res_copy.start()

    def back(angle, slot, fresh):
        for y in range(rows):
            pieces = [
                respad[slot, pl.ds(start, tcount)].reshape(flat, tile).astype(BF16)
                for start in starts(angle, y, -1)
            ]
            acc = jnp.dot(
                jnp.concatenate(pieces, axis=1), turned[angle, y], preferred_element_type=F32
            )
            grad[y] = acc if fresh else grad[y] + acc

    def take(block, slot):
        respad[slot, margin:zero_start] = block.astype(F32).reshape(tcount, depth, tile)

    back(me, 0, True)
    forward(chips - 1).wait_recv()
    take(sibres_recv[chips - 1], 1)
    back(sib, 1, False)
    for i in range(chips - 1):
        source = lax.rem(chip + chips - order[i], chips)
        same_copy(i).wait_recv()
        forward(i).start()
        take(same_recv[i], 0)
        back(2 * source + core, 0, False)
        forward(i).wait_recv()
        take(sibres_recv[i], 1)
        back(2 * source + 1 - core, 1, False)

    for y in range(rows):
        out = (base[y] - step_size * grad[y]).reshape(tcount, depth, tile)
        for t in range(tcount):
            upd_ref[:, y, t * tile : (t + 1) * tile] = out[t]
    upd_copy = pltpu.make_async_copy(upd_ref, upd_hbm, load_sem.at[n + 5])
    upd_copy.start()

    for there, copy in halos:
        pl.when(there)(copy.wait_send)
    for i in range(chips):
        sib_copy(i).wait_send()
        forward(i).wait_send()
    for i in range(chips - 1):
        chip_copy(i).wait_send()
        same_copy(i).wait_send()
    res_copy.wait()
    upd_copy.wait()


def finish(upd_in, res_in, upd_out, res_out, upd, res, sem):
    parts = sem.shape[1] - 1
    size = upd.shape[0] // parts
    pairs = [(res_in, res, res_out)]
    for i in range(parts):
        span = pl.ds(i * size, size)
        pairs.append((upd_in.at[span], upd.at[span], upd_out.at[span]))
    reads = [pltpu.make_async_copy(p[0], p[1], sem.at[0, i]) for i, p in enumerate(pairs)]
    writes = [pltpu.make_async_copy(p[1], p[2], sem.at[1, i]) for i, p in enumerate(pairs)]
    for read in reads:
        read.start()
    for read, write in zip(reads, writes):
        read.wait()
        write.start()
    for write in writes:
        write.wait()


def per_device(slabs, n, volume, measured, ray_tiles, tile_offsets, band_counts):
    depth, rows, width = volume.shape
    count, unused, band, tile, unused_2 = ray_tiles.shape
    tcount = width // tile
    flat = tcount * depth
    padded = 2 * tcount + OFFMAX + band
    chips = n // 2
    dma = pltpu.SemaphoreType.DMA
    vmem = pltpu.VMEM
    block = (flat, tile)
    shapes = (
        jax.ShapeDtypeStruct(volume.shape, F32),
        jax.ShapeDtypeStruct(measured.shape, F32),
    )
    updated, residual = pl.pallas_call(
        functools.partial(kernel, slabs, n),
        out_shape=shapes,
        in_specs=[pl.BlockSpec(memory_space=pl.ANY)] * 5,
        out_specs=(pl.BlockSpec(memory_space=pl.ANY),) * 2,
        scratch_shapes=[
            vmem(volume.shape, F32),
            vmem(measured.shape, F32),
            vmem(volume.shape, BF16),
            vmem(measured.shape, F32),
            vmem(ray_tiles.shape, BF16),
            vmem((n, rows, band * tile, tile), BF16),
            vmem(volume.shape, F32),
            vmem((rows, padded, depth, tile), F32),
            vmem(block, F32),
            vmem((chips, *block), F32),
            vmem((chips, *block), F32),
            vmem((chips - 1, *block), F32),
            vmem((chips - 1, *block), F32),
            vmem((chips - 1, *block), BF16),
            vmem((chips, *block), BF16),
            vmem(block, BF16),
            vmem((2, padded, depth, tile), F32),
            vmem((rows, *block), F32),
            vmem((rows, *block), F32),
            vmem((rows, width), F32),
            vmem((2, *block), BF16),
            vmem((2, *block), BF16),
            vmem((2, rows, width), F32),
            vmem((2, rows, width), F32),
            pltpu.SMEM(tile_offsets.shape, jnp.int32),
            pltpu.SMEM(band_counts.shape, jnp.int32),
            dma((6 + n,)),
            dma((chips,)),
            dma((chips,)),
            dma((chips - 1,)),
            dma((chips - 1,)),
            dma((chips - 1,)),
            dma((chips - 1,)),
            dma((chips,)),
            dma((chips,)),
            dma((2,)),
            dma((2,)),
            dma((2,)),
            dma((2,)),
            dma((2,)),
            dma((2,)),
        ],
        compiler_params=pltpu.CompilerParams(
            collective_id=0, has_side_effects=True, vmem_limit_bytes=60 * 1024 * 1024
        ),
        name="step",
    )(volume, measured, ray_tiles, tile_offsets, band_counts)
    return pl.pallas_call(
        finish,
        out_shape=shapes,
        in_specs=[pl.BlockSpec(memory_space=pl.ANY)] * 2,
        out_specs=(pl.BlockSpec(memory_space=pl.ANY),) * 2,
        scratch_shapes=[vmem(volume.shape, F32), vmem(measured.shape, F32), dma((2, 5))],
        compiler_params=pltpu.CompilerParams(vmem_limit_bytes=60 * 1024 * 1024),
        name="finish",
    )(updated, residual)


def solution(mesh):
    return jax.shard_map(
        functools.partial(per_device, mesh.shape["slab"], mesh.shape["angle"]),
        mesh=mesh,
        in_specs=(
            P("slab", "angle", None),
            P("angle", "slab", None),
            P(None, "angle", None, None, None),
            P(),
            P(),
        ),
        out_specs=(P("slab", "angle", None), P("angle", "slab", None)),
        check_vma=False,
    )
```

```python
import functools

import jax
import jax.numpy as jnp
from jax import lax
from jax.experimental import pallas as pl
from jax.experimental.pallas import tpu as pltpu
from jax.sharding import PartitionSpec as P

OFFMAX = 3
HALVES = 2

step_size = 0.3
smooth_weight = 0.2
smooth_floor = 0.25

F32 = jnp.float32
BF16 = jnp.bfloat16


def kernel(
    slabs,
    n,
    vol_hbm,
    meas_hbm,
    tiles_hbm,
    off_hbm,
    cnt_hbm,
    upd_hbm,
    res_hbm,
    upd_ref,
    res_ref,
    vol_in,
    meas,
    tiles,
    vol32,
    volt,
    part_own,
    sib_send,
    sib_recv,
    chip_send,
    chip_recv,
    same_recv,
    sibres_recv,
    own_res,
    respad,
    grad,
    base,
    flow_low,
    ys,
    yr,
    zr,
    cr,
    off_ref,
    cnt_ref,
    load_sem,
    sib_ssem,
    sib_rsem,
    chip_ssem,
    chip_rsem,
    same_ssem,
    same_rsem,
    sr_ssem,
    sr_rsem,
    y_ssem,
    y_rsem,
    z_ssem,
    z_rsem,
    c_ssem,
    c_rsem,
):
    depth, rows, width = vol_in.shape
    band = tiles.shape[2]
    tile = tiles.shape[3]
    tcount = width // tile
    flat = tcount * depth
    center = band // 2
    margin = OFFMAX + band
    zero_start = margin + tcount
    chips = n // 2

    slab = lax.axis_index("slab")
    me = lax.axis_index("angle")
    chip = lax.div(me, 2)
    core = lax.rem(me, 2)
    sib = me + 1 - 2 * core
    far_y = me - 1 + 2 * core
    first_row = me * rows
    barrier = pltpu.get_barrier_semaphore()

    has_far = (far_y >= 0) & (far_y < n)
    has_zp = slab + 1 < slabs
    has_zm = slab >= 1
    has_yp = me + 1 < n
    has_ym = me >= 1
    has_up = has_zp & has_ym
    has_down = has_zm & has_yp

    def greet(s, a):
        pl.semaphore_signal(barrier, inc=1, device_id=(s, a), device_id_type=pl.DeviceIdType.MESH)

    greet(slab, sib)
    for j in range(1, chips):
        greet(slab, 2 * lax.rem(chip + j, chips) + core)

    pl.when(has_far)(lambda: greet(slab, far_y))
    pl.when(has_zp)(lambda: greet(slab + 1, me))
    pl.when(has_zm)(lambda: greet(slab - 1, me))
    pl.when(has_up)(lambda: greet(slab + 1, me - 1))
    pl.when(has_down)(lambda: greet(slab - 1, me + 1))

    vol_copy = pltpu.make_async_copy(vol_hbm, vol_in, load_sem.at[0])
    vol_copy.start()
    off_copy = pltpu.make_async_copy(off_hbm, off_ref, load_sem.at[n + 2])
    off_copy.start()
    cnt_copy = pltpu.make_async_copy(cnt_hbm, cnt_ref, load_sem.at[n + 3])
    cnt_copy.start()
    order = [chips // 2] + [j for j in range(1, chips) if j != chips // 2] + [0]
    dest = [lax.rem(chip + j, chips) for j in order]
    loads = []
    for i in range(chips):
        pair = []
        for angle, slot in ((2 * dest[i] + 1 - core, 0), (2 * dest[i] + core, 1)):
            copy = pltpu.make_async_copy(
                tiles_hbm.at[angle], tiles.at[angle], load_sem.at[2 + 2 * i + slot]
            )
            copy.start()
            pair.append(copy)
        loads.append(pair)
    meas_copy = pltpu.make_async_copy(meas_hbm, meas, load_sem.at[1])
    meas_copy.start()

    volt[:, :margin] = jnp.zeros((rows, margin, depth, tile), F32)
    volt[:, zero_start:] = jnp.zeros((rows, volt.shape[1] - zero_start, depth, tile), F32)
    respad[:, :margin] = jnp.zeros((2, margin, depth, tile), F32)
    respad[:, zero_start:] = jnp.zeros((2, respad.shape[1] - zero_start, depth, tile), F32)
    vol_copy.wait()
    vol32[...] = vol_in[...].astype(F32)
    for y in range(rows):
        for t in range(tcount):
            volt[y, margin + t] = vol32[:, y, t * tile : (t + 1) * tile]

    def own_row(y):
        return volt[y, margin : margin + tcount].reshape(flat, tile)

    ys[0] = own_row(0).astype(BF16)
    ys[1] = own_row(rows - 1).astype(BF16)

    def send(src, dst, ssem, rsem, s, a):
        return pltpu.make_async_remote_copy(
            src_ref=src,
            dst_ref=dst,
            send_sem=ssem,
            recv_sem=rsem,
            device_id=(s, a),
            device_id_type=pl.DeviceIdType.MESH,
        )

    halos = (
        (has_ym, send(ys.at[0], yr.at[1], y_ssem.at[0], y_rsem.at[1], slab, me - 1)),
        (has_yp, send(ys.at[1], yr.at[0], y_ssem.at[1], y_rsem.at[0], slab, me + 1)),
        (has_zm, send(vol32.at[0], zr.at[1], z_ssem.at[0], z_rsem.at[1], slab - 1, me)),
        (has_zp, send(vol32.at[depth - 1], zr.at[0], z_ssem.at[1], z_rsem.at[0], slab + 1, me)),
        (has_down, send(vol32.at[0], cr.at[1], c_ssem.at[0], c_rsem.at[1], slab - 1, me + 1)),
        (has_up, send(vol32.at[depth - 1], cr.at[0], c_ssem.at[1], c_rsem.at[0], slab + 1, me - 1)),
    )
    arrivals = (
        (has_yp, yr.at[1], send(ys.at[0], yr.at[1], y_ssem.at[0], y_rsem.at[1], slab, me + 1)),
        (has_ym, yr.at[0], send(ys.at[1], yr.at[0], y_ssem.at[1], y_rsem.at[0], slab, me - 1)),
        (has_zp, zr.at[1], send(vol32.at[0], zr.at[1], z_ssem.at[0], z_rsem.at[1], slab + 1, me)),
        (has_zm, zr.at[0], send(vol32.at[depth - 1], zr.at[0], z_ssem.at[1], z_rsem.at[0], slab - 1, me)),
        (has_up, cr.at[1], send(vol32.at[0], cr.at[1], c_ssem.at[0], c_rsem.at[1], slab + 1, me - 1)),
        (has_down, cr.at[0], send(vol32.at[depth - 1], cr.at[0], c_ssem.at[1], c_rsem.at[0], slab - 1, me + 1)),
    )
    def starts(angle, y, sign):
        found = []
        for k in range(band):
            shift = off_ref[angle, first_row + y] + (k - center)
            used = cnt_ref[angle, first_row + y] > k
            found.append(jnp.where(used, margin + sign * shift, zero_start))
        return found

    def view(angle):
        pieces = []
        for y in range(rows):
            for start in starts(angle, y, 1):
                pieces.append(volt[y, pl.ds(start, tcount)].reshape(flat, tile).astype(BF16))
        weights = tiles[angle].reshape(rows * band * tile, tile)
        return jnp.dot(jnp.concatenate(pieces, axis=1), weights, preferred_element_type=F32)

    def sib_copy(i):
        return send(sib_send.at[i], sib_recv.at[i], sib_ssem.at[i], sib_rsem.at[i], slab, sib)

    part = flat // HALVES

    def span(h):
        return pl.ds(h * part, part)

    def chip_copy(i, h):
        return send(
            chip_send.at[i, span(h)],
            chip_recv.at[i, span(h)],
            chip_ssem.at[i, h],
            chip_rsem.at[i, h],
            slab,
            2 * dest[i] + core,
        )

    def for_sibling(i):
        loads[i][0].wait()
        sib_send[i] = view(2 * dest[i] + 1 - core)

    off_copy.wait()
    cnt_copy.wait()
    for_sibling(0)

    one = jnp.int32(1)
    none = jnp.int32(0)
    expect = jnp.int32(chips)
    for there in (has_far, has_zp, has_zm, has_up, has_down):
        expect = expect + jnp.where(there, one, none)
    pl.semaphore_wait(barrier, expect)

    sib_copy(0).start()
    for there, copy in halos:
        pl.when(there)(copy.start)

    for i in range(chips):
        if i + 1 < chips:
            for_sibling(i + 1)
            sib_copy(i + 1).start()
        loads[i][1].wait()
        part_own[...] = view(2 * dest[i] + core)
        sib_copy(i).wait_recv()
        if i + 1 < chips:
            chip_send[i] = part_own[...] + sib_recv[i]
            chip_copy(i, 0).start()
        else:
            part_own[...] = part_own[...] + sib_recv[i]

    for h in range(1, HALVES):
        for i in range(chips - 1):
            chip_copy(i, h).start()

    for there, buffer, copy in arrivals:
        pl.when(there)(copy.wait_recv)

        @pl.when(jnp.logical_not(there))
        def _(buffer=buffer):
            buffer[...] = jnp.zeros(buffer.shape, buffer.dtype)

    lane = lax.broadcasted_iota(jnp.int32, (flat + depth, tile), 1)
    level = lax.rem(lax.broadcasted_iota(jnp.int32, (flat + depth, tile), 0), depth)
    zeros_tile = jnp.zeros((depth, tile), F32)

    low = zr[0]
    low_y = jnp.concatenate([low[1:], cr[0][:1]], axis=0)
    low_lane = lax.broadcasted_iota(jnp.int32, (rows, width), 1)
    low_x = jnp.where(low_lane == width - 1, 0.0, pltpu.roll(low, width - 1, 1))
    lz, ly, lx = vol32[0] - low, low_y - low, low_x - low
    flow_low[...] = lz * lax.rsqrt(lz * lz + ly * ly + lx * lx + smooth_floor)

    def field_row(y):
        if 0 <= y < rows:
            return volt[y, margin - 1 : margin + tcount + 1].reshape(flat + 2 * depth, tile)
        inner = yr[0 if y < 0 else 1].astype(F32)
        return jnp.concatenate([zeros_tile, inner, zeros_tile], axis=0)

    def spread_row(ref, row):
        return [
            jnp.broadcast_to(ref[row : row + 1, t * tile : (t + 1) * tile], (depth, tile))
            for t in range(tcount)
        ]

    def flow(y):
        wide = field_row(y)
        here = wide[: flat + depth]
        rolled = pltpu.roll(wide, tile - 1, 1)
        dx = jnp.where(lane == tile - 1, rolled[depth:], rolled[: flat + depth]) - here
        dy = field_row(y + 1)[: flat + depth] - here
        top = spread_row(zr.at[1], y) if y >= 0 else spread_row(cr.at[1], rows - 1)
        top = jnp.concatenate([zeros_tile] + top, axis=0)
        dz = jnp.where(level == depth - 1, top, pltpu.roll(here, flat + depth - 1, 0)) - here
        inv = lax.rsqrt(dz * dz + dy * dy + dx * dx + smooth_floor)
        return dz * inv, dy * inv, dx * inv

    before = flow(-1)[1][depth:]
    for y in range(rows):
        fz, fy, fx = flow(y)
        fz, fy = fz[depth:], fy[depth:]
        under = jnp.concatenate(spread_row(flow_low, y), axis=0)
        div = fz - jnp.where(level[:flat] == 0, under, pltpu.roll(fz, 1, 0))
        div = div + (fy - before)
        rolled = pltpu.roll(fx, 1, 1)
        div = div + (fx[depth:] - jnp.where(lane[:flat] == 0, rolled[:flat], rolled[depth:]))
        base[y] = own_row(y) + step_size * smooth_weight * div
        before = fy

    def same_copy(i, h):
        return send(
            own_res.at[span(h)],
            same_recv.at[i, span(h)],
            same_ssem.at[i, h],
            same_rsem.at[i, h],
            slab,
            2 * dest[i] + core,
        )

    def forward(i, h):
        src = own_res.at[span(h)] if i == chips - 1 else same_recv.at[i, span(h)]
        return send(src, sibres_recv.at[i, span(h)], sr_ssem.at[i, h], sr_rsem.at[i, h], slab, sib)

    meas_copy.wait()
    for h in range(HALVES):
        total = part_own[span(h)]
        for i in range(chips - 1):
            chip_copy(i, h).wait_recv()
            total = total + chip_recv[i, span(h)]
        total = total.reshape(tcount // HALVES, depth, tile)
        first = h * (tcount // HALVES)
        for j in range(tcount // HALVES):
            t = first + j
            here = total[j] - meas[0, :, t * tile : (t + 1) * tile]
            res_ref[0, :, t * tile : (t + 1) * tile] = here
            respad[0, margin + t] = here.astype(BF16).astype(F32)
        block = respad[0, margin + first : margin + first + tcount // HALVES]
        own_res[span(h)] = block.reshape(part, tile).astype(BF16)
        for i in range(chips - 1):
            same_copy(i, h).start()
        forward(chips - 1, h).start()
    res_copy = pltpu.make_async_copy(res_ref, res_hbm, load_sem.at[n + 4])
    res_copy.start()

    def back(angle, slot, fresh):
        for y in range(rows):
            pieces = [
                respad[slot, pl.ds(start, tcount)].reshape(flat, tile).astype(BF16)
                for start in starts(angle, y, -1)
            ]
            weights = jnp.concatenate([tiles[angle, y, k] for k in range(band)], axis=1)
            acc = lax.dot_general(
                jnp.concatenate(pieces, axis=1),
                weights,
                (((1,), (1,)), ((), ())),
                preferred_element_type=F32,
            )
            grad[y] = acc if fresh else grad[y] + acc

    def take(block, slot):
        respad[slot, margin:zero_start] = block.astype(F32).reshape(tcount, depth, tile)

    source = [lax.rem(chip + chips - j, chips) for j in order]

    def pass_on(i, h):
        same_copy(i, h).wait_recv()
        forward(i, h).start()

    def from_sibling(i):
        for h in range(HALVES):
            forward(i, h).wait_recv()
        take(sibres_recv[i], 1)
        back(2 * source[i] + 1 - core, 1, False)

    back(me, 0, True)
    for h in range(HALVES - 1):
        for i in range(chips - 1):
            pass_on(i, h)
    from_sibling(chips - 1)
    for i in range(chips - 1):
        pass_on(i, HALVES - 1)
        take(same_recv[i], 0)
        back(2 * source[i] + core, 0, False)
        if i > 0:
            from_sibling(i - 1)
    from_sibling(chips - 2)

    for y in range(rows):
        out = (base[y] - step_size * grad[y]).reshape(tcount, depth, tile)
        for t in range(tcount):
            upd_ref[:, y, t * tile : (t + 1) * tile] = out[t]
    upd_copy = pltpu.make_async_copy(upd_ref, upd_hbm, load_sem.at[n + 5])
    upd_copy.start()

    for there, copy in halos:
        pl.when(there)(copy.wait_send)
    for i in range(chips):
        sib_copy(i).wait_send()
        for h in range(HALVES):
            forward(i, h).wait_send()
            if i + 1 < chips:
                chip_copy(i, h).wait_send()
                same_copy(i, h).wait_send()
    res_copy.wait()
    upd_copy.wait()


def finish(upd_in, res_in, upd_out, res_out, upd, res, sem):
    parts = sem.shape[1] - 1
    size = upd.shape[0] // parts
    pairs = [(res_in, res, res_out)]
    for i in range(parts):
        span = pl.ds(i * size, size)
        pairs.append((upd_in.at[span], upd.at[span], upd_out.at[span]))
    reads = [pltpu.make_async_copy(p[0], p[1], sem.at[0, i]) for i, p in enumerate(pairs)]
    writes = [pltpu.make_async_copy(p[1], p[2], sem.at[1, i]) for i, p in enumerate(pairs)]
    for read in reads:
        read.start()
    for read, write in zip(reads, writes):
        read.wait()
        write.start()
    for write in writes:
        write.wait()


def per_device(slabs, n, volume, measured, ray_tiles, tile_offsets, band_counts):
    depth, rows, width = volume.shape
    count, unused, band, tile, unused_2 = ray_tiles.shape
    tcount = width // tile
    flat = tcount * depth
    padded = 2 * tcount + OFFMAX + band
    chips = n // 2
    dma = pltpu.SemaphoreType.DMA
    vmem = pltpu.VMEM
    block = (flat, tile)
    shapes = (
        jax.ShapeDtypeStruct(volume.shape, F32),
        jax.ShapeDtypeStruct(measured.shape, F32),
    )
    updated, residual = pl.pallas_call(
        functools.partial(kernel, slabs, n),
        out_shape=shapes,
        in_specs=[pl.BlockSpec(memory_space=pl.ANY)] * 5,
        out_specs=(pl.BlockSpec(memory_space=pl.ANY),) * 2,
        scratch_shapes=[
            vmem(volume.shape, F32),
            vmem(measured.shape, F32),
            vmem(volume.shape, BF16),
            vmem(measured.shape, F32),
            vmem(ray_tiles.shape, BF16),
            vmem(volume.shape, F32),
            vmem((rows, padded, depth, tile), F32),
            vmem(block, F32),
            vmem((chips, *block), F32),
            vmem((chips, *block), F32),
            vmem((chips - 1, *block), F32),
            vmem((chips - 1, *block), F32),
            vmem((chips - 1, *block), BF16),
            vmem((chips, *block), BF16),
            vmem(block, BF16),
            vmem((2, padded, depth, tile), F32),
            vmem((rows, *block), F32),
            vmem((rows, *block), F32),
            vmem((rows, width), F32),
            vmem((2, *block), BF16),
            vmem((2, *block), BF16),
            vmem((2, rows, width), F32),
            vmem((2, rows, width), F32),
            pltpu.SMEM(tile_offsets.shape, jnp.int32),
            pltpu.SMEM(band_counts.shape, jnp.int32),
            dma((6 + n,)),
            dma((chips,)),
            dma((chips,)),
            dma((chips - 1, HALVES)),
            dma((chips - 1, HALVES)),
            dma((chips - 1, HALVES)),
            dma((chips - 1, HALVES)),
            dma((chips, HALVES)),
            dma((chips, HALVES)),
            dma((2,)),
            dma((2,)),
            dma((2,)),
            dma((2,)),
            dma((2,)),
            dma((2,)),
        ],
        compiler_params=pltpu.CompilerParams(
            collective_id=0, has_side_effects=True, vmem_limit_bytes=60 * 1024 * 1024
        ),
        name="step",
    )(volume, measured, ray_tiles, tile_offsets, band_counts)
    return pl.pallas_call(
        finish,
        out_shape=shapes,
        in_specs=[pl.BlockSpec(memory_space=pl.ANY)] * 2,
        out_specs=(pl.BlockSpec(memory_space=pl.ANY),) * 2,
        scratch_shapes=[vmem(volume.shape, F32), vmem(measured.shape, F32), dma((2, 5))],
        compiler_params=pltpu.CompilerParams(vmem_limit_bytes=60 * 1024 * 1024),
        name="finish",
    )(updated, residual)


def solution(mesh):
    return jax.shard_map(
        functools.partial(per_device, mesh.shape["slab"], mesh.shape["angle"]),
        mesh=mesh,
        in_specs=(
            P("slab", "angle", None),
            P("angle", "slab", None),
            P(None, "angle", None, None, None),
            P(),
            P(),
        ),
        out_specs=(P("slab", "angle", None), P("angle", "slab", None)),
        check_vma=False,
    )
```

```python
import functools

import jax
import jax.numpy as jnp
from jax import lax
from jax.experimental import pallas as pl
from jax.experimental.pallas import tpu as pltpu
from jax.sharding import PartitionSpec as P

OFFMAX = 3
PARTS = 4

step_size = 0.3
smooth_weight = 0.2
smooth_floor = 0.25

F32 = jnp.float32
BF16 = jnp.bfloat16


def kernel(
    slabs,
    n,
    vol_hbm,
    meas_hbm,
    tiles_hbm,
    off_hbm,
    cnt_hbm,
    upd_hbm,
    res_hbm,
    upd_ref,
    res_ref,
    vol_in,
    meas,
    tiles,
    vol32,
    volt,
    part_own,
    sib_send,
    sib_recv,
    chip_send,
    chip_recv,
    same_recv,
    sibres_recv,
    own_res,
    respad,
    grad,
    base,
    flow_low,
    ys,
    yr,
    zr,
    cr,
    off_ref,
    cnt_ref,
    load_sem,
    sib_ssem,
    sib_rsem,
    chip_ssem,
    chip_rsem,
    same_ssem,
    same_rsem,
    sr_ssem,
    sr_rsem,
    y_ssem,
    y_rsem,
    z_ssem,
    z_rsem,
    c_ssem,
    c_rsem,
):
    depth, rows, width = vol_in.shape
    band = tiles.shape[2]
    tile = tiles.shape[3]
    tcount = width // tile
    flat = tcount * depth
    center = band // 2
    margin = OFFMAX + band
    zero_start = margin + tcount
    chips = n // 2

    slab = lax.axis_index("slab")
    me = lax.axis_index("angle")
    chip = lax.div(me, 2)
    core = lax.rem(me, 2)
    sib = me + 1 - 2 * core
    far_y = me - 1 + 2 * core
    first_row = me * rows
    barrier = pltpu.get_barrier_semaphore()

    has_far = (far_y >= 0) & (far_y < n)
    has_zp = slab + 1 < slabs
    has_zm = slab >= 1
    has_yp = me + 1 < n
    has_ym = me >= 1
    has_up = has_zp & has_ym
    has_down = has_zm & has_yp

    def greet(s, a):
        pl.semaphore_signal(barrier, inc=1, device_id=(s, a), device_id_type=pl.DeviceIdType.MESH)

    greet(slab, sib)
    for j in range(1, chips):
        greet(slab, 2 * lax.rem(chip + j, chips) + core)

    pl.when(has_far)(lambda: greet(slab, far_y))
    pl.when(has_zp)(lambda: greet(slab + 1, me))
    pl.when(has_zm)(lambda: greet(slab - 1, me))
    pl.when(has_up)(lambda: greet(slab + 1, me - 1))
    pl.when(has_down)(lambda: greet(slab - 1, me + 1))

    vol_copy = pltpu.make_async_copy(vol_hbm, vol_in, load_sem.at[0])
    vol_copy.start()
    off_copy = pltpu.make_async_copy(off_hbm, off_ref, load_sem.at[n + 2])
    off_copy.start()
    cnt_copy = pltpu.make_async_copy(cnt_hbm, cnt_ref, load_sem.at[n + 3])
    cnt_copy.start()
    order = [chips // 2] + [j for j in range(1, chips) if j != chips // 2] + [0]
    dest = [lax.rem(chip + j, chips) for j in order]
    loads = []
    for i in range(chips):
        pair = []
        for angle, slot in ((2 * dest[i] + 1 - core, 0), (2 * dest[i] + core, 1)):
            copy = pltpu.make_async_copy(
                tiles_hbm.at[angle], tiles.at[angle], load_sem.at[2 + 2 * i + slot]
            )
            copy.start()
            pair.append(copy)
        loads.append(pair)
    meas_copy = pltpu.make_async_copy(meas_hbm, meas, load_sem.at[1])
    meas_copy.start()

    volt[:, :margin] = jnp.zeros((rows, margin, depth, tile), F32)
    volt[:, zero_start:] = jnp.zeros((rows, volt.shape[1] - zero_start, depth, tile), F32)
    respad[:, :margin] = jnp.zeros((2, margin, depth, tile), F32)
    respad[:, zero_start:] = jnp.zeros((2, respad.shape[1] - zero_start, depth, tile), F32)
    vol_copy.wait()
    vol32[...] = vol_in[...].astype(F32)
    for y in range(rows):
        for t in range(tcount):
            volt[y, margin + t] = vol32[:, y, t * tile : (t + 1) * tile]

    def own_row(y):
        return volt[y, margin : margin + tcount].reshape(flat, tile)

    ys[0] = own_row(0).astype(BF16)
    ys[1] = own_row(rows - 1).astype(BF16)

    def send(src, dst, ssem, rsem, s, a):
        return pltpu.make_async_remote_copy(
            src_ref=src,
            dst_ref=dst,
            send_sem=ssem,
            recv_sem=rsem,
            device_id=(s, a),
            device_id_type=pl.DeviceIdType.MESH,
        )

    halos = (
        (has_ym, send(ys.at[0], yr.at[1], y_ssem.at[0], y_rsem.at[1], slab, me - 1)),
        (has_yp, send(ys.at[1], yr.at[0], y_ssem.at[1], y_rsem.at[0], slab, me + 1)),
        (has_zm, send(vol32.at[0], zr.at[1], z_ssem.at[0], z_rsem.at[1], slab - 1, me)),
        (has_zp, send(vol32.at[depth - 1], zr.at[0], z_ssem.at[1], z_rsem.at[0], slab + 1, me)),
        (has_down, send(vol32.at[0], cr.at[1], c_ssem.at[0], c_rsem.at[1], slab - 1, me + 1)),
        (has_up, send(vol32.at[depth - 1], cr.at[0], c_ssem.at[1], c_rsem.at[0], slab + 1, me - 1)),
    )
    arrivals = (
        (has_yp, yr.at[1], send(ys.at[0], yr.at[1], y_ssem.at[0], y_rsem.at[1], slab, me + 1)),
        (has_ym, yr.at[0], send(ys.at[1], yr.at[0], y_ssem.at[1], y_rsem.at[0], slab, me - 1)),
        (has_zp, zr.at[1], send(vol32.at[0], zr.at[1], z_ssem.at[0], z_rsem.at[1], slab + 1, me)),
        (has_zm, zr.at[0], send(vol32.at[depth - 1], zr.at[0], z_ssem.at[1], z_rsem.at[0], slab - 1, me)),
        (has_up, cr.at[1], send(vol32.at[0], cr.at[1], c_ssem.at[0], c_rsem.at[1], slab + 1, me - 1)),
        (has_down, cr.at[0], send(vol32.at[depth - 1], cr.at[0], c_ssem.at[1], c_rsem.at[0], slab - 1, me + 1)),
    )
    def starts(angle, y, sign):
        found = []
        for k in range(band):
            shift = off_ref[angle, first_row + y] + (k - center)
            used = cnt_ref[angle, first_row + y] > k
            found.append(jnp.where(used, margin + sign * shift, zero_start))
        return found

    def view(angle):
        pieces = []
        for y in range(rows):
            for start in starts(angle, y, 1):
                pieces.append(volt[y, pl.ds(start, tcount)].reshape(flat, tile).astype(BF16))
        weights = tiles[angle].reshape(rows * band * tile, tile)
        return jnp.dot(jnp.concatenate(pieces, axis=1), weights, preferred_element_type=F32)

    def sib_copy(i):
        return send(sib_send.at[i], sib_recv.at[i], sib_ssem.at[i], sib_rsem.at[i], slab, sib)

    part = flat // PARTS

    def span(h):
        return pl.ds(h * part, part)

    def chip_copy(i, h):
        return send(
            chip_send.at[i, span(h)],
            chip_recv.at[i, span(h)],
            chip_ssem.at[i, h],
            chip_rsem.at[i, h],
            slab,
            2 * dest[i] + core,
        )

    def for_sibling(i):
        loads[i][0].wait()
        sib_send[i] = view(2 * dest[i] + 1 - core)

    off_copy.wait()
    cnt_copy.wait()
    for_sibling(0)

    one = jnp.int32(1)
    none = jnp.int32(0)
    expect = jnp.int32(chips)
    for there in (has_far, has_zp, has_zm, has_up, has_down):
        expect = expect + jnp.where(there, one, none)
    pl.semaphore_wait(barrier, expect)

    sib_copy(0).start()
    for there, copy in halos:
        pl.when(there)(copy.start)

    for i in range(chips):
        if i + 1 < chips:
            for_sibling(i + 1)
            sib_copy(i + 1).start()
        loads[i][1].wait()
        part_own[...] = view(2 * dest[i] + core)
        sib_copy(i).wait_recv()
        if i + 1 < chips:
            chip_send[i] = part_own[...] + sib_recv[i]
            chip_copy(i, 0).start()
        else:
            part_own[...] = part_own[...] + sib_recv[i]

    for h in range(1, PARTS):
        for i in range(chips - 1):
            chip_copy(i, h).start()

    for there, buffer, copy in arrivals:
        pl.when(there)(copy.wait_recv)

        @pl.when(jnp.logical_not(there))
        def _(buffer=buffer):
            buffer[...] = jnp.zeros(buffer.shape, buffer.dtype)

    lane = lax.broadcasted_iota(jnp.int32, (flat + depth, tile), 1)
    level = lax.rem(lax.broadcasted_iota(jnp.int32, (flat + depth, tile), 0), depth)
    zeros_tile = jnp.zeros((depth, tile), F32)

    low = zr[0]
    low_y = jnp.concatenate([low[1:], cr[0][:1]], axis=0)
    low_lane = lax.broadcasted_iota(jnp.int32, (rows, width), 1)
    low_x = jnp.where(low_lane == width - 1, 0.0, pltpu.roll(low, width - 1, 1))
    lz, ly, lx = vol32[0] - low, low_y - low, low_x - low
    flow_low[...] = lz * lax.rsqrt(lz * lz + ly * ly + lx * lx + smooth_floor)

    def field_row(y):
        if 0 <= y < rows:
            return volt[y, margin - 1 : margin + tcount + 1].reshape(flat + 2 * depth, tile)
        inner = yr[0 if y < 0 else 1].astype(F32)
        return jnp.concatenate([zeros_tile, inner, zeros_tile], axis=0)

    def spread_row(ref, row):
        return [
            jnp.broadcast_to(ref[row : row + 1, t * tile : (t + 1) * tile], (depth, tile))
            for t in range(tcount)
        ]

    def flow(y):
        wide = field_row(y)
        here = wide[: flat + depth]
        rolled = pltpu.roll(wide, tile - 1, 1)
        dx = jnp.where(lane == tile - 1, rolled[depth:], rolled[: flat + depth]) - here
        dy = field_row(y + 1)[: flat + depth] - here
        top = spread_row(zr.at[1], y) if y >= 0 else spread_row(cr.at[1], rows - 1)
        top = jnp.concatenate([zeros_tile] + top, axis=0)
        dz = jnp.where(level == depth - 1, top, pltpu.roll(here, flat + depth - 1, 0)) - here
        inv = lax.rsqrt(dz * dz + dy * dy + dx * dx + smooth_floor)
        return dz * inv, dy * inv, dx * inv

    before = flow(-1)[1][depth:]
    for y in range(rows):
        fz, fy, fx = flow(y)
        fz, fy = fz[depth:], fy[depth:]
        under = jnp.concatenate(spread_row(flow_low, y), axis=0)
        div = fz - jnp.where(level[:flat] == 0, under, pltpu.roll(fz, 1, 0))
        div = div + (fy - before)
        rolled = pltpu.roll(fx, 1, 1)
        div = div + (fx[depth:] - jnp.where(lane[:flat] == 0, rolled[:flat], rolled[depth:]))
        base[y] = own_row(y) + step_size * smooth_weight * div
        before = fy

    def same_copy(i, h):
        return send(
            own_res.at[span(h)],
            same_recv.at[i, span(h)],
            same_ssem.at[i, h],
            same_rsem.at[i, h],
            slab,
            2 * dest[i] + core,
        )

    def forward(i, h):
        src = own_res.at[span(h)] if i == chips - 1 else same_recv.at[i, span(h)]
        return send(src, sibres_recv.at[i, span(h)], sr_ssem.at[i, h], sr_rsem.at[i, h], slab, sib)

    meas_copy.wait()
    for h in range(PARTS):
        total = part_own[span(h)]
        for i in range(chips - 1):
            chip_copy(i, h).wait_recv()
            total = total + chip_recv[i, span(h)]
        total = total.reshape(tcount // PARTS, depth, tile)
        first = h * (tcount // PARTS)
        for j in range(tcount // PARTS):
            t = first + j
            here = total[j] - meas[0, :, t * tile : (t + 1) * tile]
            res_ref[0, :, t * tile : (t + 1) * tile] = here
            respad[0, margin + t] = here.astype(BF16).astype(F32)
        block = respad[0, margin + first : margin + first + tcount // PARTS]
        own_res[span(h)] = block.reshape(part, tile).astype(BF16)
        for i in range(chips - 1):
            same_copy(i, h).start()
        forward(chips - 1, h).start()
    res_copy = pltpu.make_async_copy(res_ref, res_hbm, load_sem.at[n + 4])
    res_copy.start()

    def back(angle, slot, fresh):
        for y in range(rows):
            pieces = [
                respad[slot, pl.ds(start, tcount)].reshape(flat, tile).astype(BF16)
                for start in starts(angle, y, -1)
            ]
            weights = jnp.concatenate([tiles[angle, y, k] for k in range(band)], axis=1)
            acc = lax.dot_general(
                jnp.concatenate(pieces, axis=1),
                weights,
                (((1,), (1,)), ((), ())),
                preferred_element_type=F32,
            )
            grad[y] = acc if fresh else grad[y] + acc

    def take(block, slot):
        respad[slot, margin:zero_start] = block.astype(F32).reshape(tcount, depth, tile)

    source = [lax.rem(chip + chips - j, chips) for j in order]

    def pass_on(i, h):
        same_copy(i, h).wait_recv()
        forward(i, h).start()

    def from_sibling(i):
        for h in range(PARTS):
            forward(i, h).wait_recv()
        take(sibres_recv[i], 1)
        back(2 * source[i] + 1 - core, 1, False)

    back(me, 0, True)
    for h in range(PARTS - 1):
        for i in range(chips - 1):
            pass_on(i, h)
    from_sibling(chips - 1)
    for i in range(chips - 1):
        pass_on(i, PARTS - 1)
        take(same_recv[i], 0)
        back(2 * source[i] + core, 0, False)
        if i > 0:
            from_sibling(i - 1)
    from_sibling(chips - 2)

    for y in range(rows):
        out = (base[y] - step_size * grad[y]).reshape(tcount, depth, tile)
        for t in range(tcount):
            upd_ref[:, y, t * tile : (t + 1) * tile] = out[t]
    upd_copy = pltpu.make_async_copy(upd_ref, upd_hbm, load_sem.at[n + 5])
    upd_copy.start()

    for there, copy in halos:
        pl.when(there)(copy.wait_send)
    for i in range(chips):
        sib_copy(i).wait_send()
        for h in range(PARTS):
            forward(i, h).wait_send()
            if i + 1 < chips:
                chip_copy(i, h).wait_send()
                same_copy(i, h).wait_send()
    res_copy.wait()
    upd_copy.wait()


def finish(upd_in, res_in, upd_out, res_out, upd, res, sem):
    parts = sem.shape[1] - 1
    size = upd.shape[0] // parts
    pairs = [(res_in, res, res_out)]
    for i in range(parts):
        span = pl.ds(i * size, size)
        pairs.append((upd_in.at[span], upd.at[span], upd_out.at[span]))
    reads = [pltpu.make_async_copy(p[0], p[1], sem.at[0, i]) for i, p in enumerate(pairs)]
    writes = [pltpu.make_async_copy(p[1], p[2], sem.at[1, i]) for i, p in enumerate(pairs)]
    for read in reads:
        read.start()
    for read, write in zip(reads, writes):
        read.wait()
        write.start()
    for write in writes:
        write.wait()


def per_device(slabs, n, volume, measured, ray_tiles, tile_offsets, band_counts):
    depth, rows, width = volume.shape
    count, unused, band, tile, unused_2 = ray_tiles.shape
    tcount = width // tile
    flat = tcount * depth
    padded = 2 * tcount + OFFMAX + band
    chips = n // 2
    dma = pltpu.SemaphoreType.DMA
    vmem = pltpu.VMEM
    block = (flat, tile)
    shapes = (
        jax.ShapeDtypeStruct(volume.shape, F32),
        jax.ShapeDtypeStruct(measured.shape, F32),
    )
    updated, residual = pl.pallas_call(
        functools.partial(kernel, slabs, n),
        out_shape=shapes,
        in_specs=[pl.BlockSpec(memory_space=pl.ANY)] * 5,
        out_specs=(pl.BlockSpec(memory_space=pl.ANY),) * 2,
        scratch_shapes=[
            vmem(volume.shape, F32),
            vmem(measured.shape, F32),
            vmem(volume.shape, BF16),
            vmem(measured.shape, F32),
            vmem(ray_tiles.shape, BF16),
            vmem(volume.shape, F32),
            vmem((rows, padded, depth, tile), F32),
            vmem(block, F32),
            vmem((chips, *block), F32),
            vmem((chips, *block), F32),
            vmem((chips - 1, *block), F32),
            vmem((chips - 1, *block), F32),
            vmem((chips - 1, *block), BF16),
            vmem((chips, *block), BF16),
            vmem(block, BF16),
            vmem((2, padded, depth, tile), F32),
            vmem((rows, *block), F32),
            vmem((rows, *block), F32),
            vmem((rows, width), F32),
            vmem((2, *block), BF16),
            vmem((2, *block), BF16),
            vmem((2, rows, width), F32),
            vmem((2, rows, width), F32),
            pltpu.SMEM(tile_offsets.shape, jnp.int32),
            pltpu.SMEM(band_counts.shape, jnp.int32),
            dma((6 + n,)),
            dma((chips,)),
            dma((chips,)),
            dma((chips - 1, PARTS)),
            dma((chips - 1, PARTS)),
            dma((chips - 1, PARTS)),
            dma((chips - 1, PARTS)),
            dma((chips, PARTS)),
            dma((chips, PARTS)),
            dma((2,)),
            dma((2,)),
            dma((2,)),
            dma((2,)),
            dma((2,)),
            dma((2,)),
        ],
        compiler_params=pltpu.CompilerParams(
            collective_id=0, has_side_effects=True, vmem_limit_bytes=60 * 1024 * 1024
        ),
        name="step",
    )(volume, measured, ray_tiles, tile_offsets, band_counts)
    return pl.pallas_call(
        finish,
        out_shape=shapes,
        in_specs=[pl.BlockSpec(memory_space=pl.ANY)] * 2,
        out_specs=(pl.BlockSpec(memory_space=pl.ANY),) * 2,
        scratch_shapes=[vmem(volume.shape, F32), vmem(measured.shape, F32), dma((2, 5))],
        compiler_params=pltpu.CompilerParams(vmem_limit_bytes=60 * 1024 * 1024),
        name="finish",
    )(updated, residual)


def solution(mesh):
    return jax.shard_map(
        functools.partial(per_device, mesh.shape["slab"], mesh.shape["angle"]),
        mesh=mesh,
        in_specs=(
            P("slab", "angle", None),
            P("angle", "slab", None),
            P(None, "angle", None, None, None),
            P(),
            P(),
        ),
        out_specs=(P("slab", "angle", None), P("angle", "slab", None)),
        check_vma=False,
    )
```

```python
import functools

import jax
import jax.numpy as jnp
from jax import lax
from jax.experimental import pallas as pl
from jax.experimental.pallas import tpu as pltpu
from jax.sharding import PartitionSpec as P

OFFMAX = 3
HALVES = 2

step_size = 0.3
smooth_weight = 0.2
smooth_floor = 0.25

F32 = jnp.float32
BF16 = jnp.bfloat16


def kernel(
    slabs,
    n,
    vol_hbm,
    meas_hbm,
    tiles_hbm,
    off_hbm,
    cnt_hbm,
    upd_hbm,
    res_hbm,
    upd_ref,
    res_ref,
    vol_in,
    meas,
    tiles,
    vol32,
    volt,
    part_own,
    sib_send,
    sib_recv,
    chip_send,
    chip_recv,
    same_recv,
    sibres_recv,
    own_res,
    respad,
    grad,
    base,
    flow_low,
    ys,
    yr,
    zr,
    cr,
    off_ref,
    cnt_ref,
    load_sem,
    sib_ssem,
    sib_rsem,
    chip_ssem,
    chip_rsem,
    same_ssem,
    same_rsem,
    sr_ssem,
    sr_rsem,
    y_ssem,
    y_rsem,
    z_ssem,
    z_rsem,
    c_ssem,
    c_rsem,
):
    depth, rows, width = vol_in.shape
    band = tiles.shape[2]
    tile = tiles.shape[3]
    tcount = width // tile
    flat = tcount * depth
    center = band // 2
    margin = OFFMAX + band
    zero_start = margin + tcount
    chips = n // 2

    slab = lax.axis_index("slab")
    me = lax.axis_index("angle")
    chip = lax.div(me, 2)
    core = lax.rem(me, 2)
    sib = me + 1 - 2 * core
    far_y = me - 1 + 2 * core
    first_row = me * rows
    barrier = pltpu.get_barrier_semaphore()

    has_far = (far_y >= 0) & (far_y < n)
    has_zp = slab + 1 < slabs
    has_zm = slab >= 1
    has_yp = me + 1 < n
    has_ym = me >= 1
    has_up = has_zp & has_ym
    has_down = has_zm & has_yp

    def greet(s, a):
        pl.semaphore_signal(barrier, inc=1, device_id=(s, a), device_id_type=pl.DeviceIdType.MESH)

    greet(slab, sib)
    for j in range(1, chips):
        greet(slab, 2 * lax.rem(chip + j, chips) + core)

    pl.when(has_far)(lambda: greet(slab, far_y))
    pl.when(has_zp)(lambda: greet(slab + 1, me))
    pl.when(has_zm)(lambda: greet(slab - 1, me))
    pl.when(has_up)(lambda: greet(slab + 1, me - 1))
    pl.when(has_down)(lambda: greet(slab - 1, me + 1))

    vol_copy = pltpu.make_async_copy(vol_hbm, vol_in, load_sem.at[0])
    vol_copy.start()
    off_copy = pltpu.make_async_copy(off_hbm, off_ref, load_sem.at[n + 2])
    off_copy.start()
    cnt_copy = pltpu.make_async_copy(cnt_hbm, cnt_ref, load_sem.at[n + 3])
    cnt_copy.start()
    order = [chips // 2] + [j for j in range(1, chips) if j != chips // 2] + [0]
    dest = [lax.rem(chip + j, chips) for j in order]
    source = [lax.rem(chip + chips - j, chips) for j in order]
    if chips == 4:
        dest = [lax.rem(chip + 2, 4), 3 - chip, chip + 1 - 2 * lax.rem(chip, 2), chip]
        source = dest
    loads = []
    for i in range(chips):
        pair = []
        for angle, slot in ((2 * dest[i] + 1 - core, 0), (2 * dest[i] + core, 1)):
            copy = pltpu.make_async_copy(
                tiles_hbm.at[angle], tiles.at[angle], load_sem.at[2 + 2 * i + slot]
            )
            copy.start()
            pair.append(copy)
        loads.append(pair)
    meas_copy = pltpu.make_async_copy(meas_hbm, meas, load_sem.at[1])
    meas_copy.start()

    volt[:, :margin] = jnp.zeros((rows, margin, depth, tile), F32)
    volt[:, zero_start:] = jnp.zeros((rows, volt.shape[1] - zero_start, depth, tile), F32)
    respad[:, :margin] = jnp.zeros((2, margin, depth, tile), F32)
    respad[:, zero_start:] = jnp.zeros((2, respad.shape[1] - zero_start, depth, tile), F32)
    vol_copy.wait()
    vol32[...] = vol_in[...].astype(F32)
    for y in range(rows):
        for t in range(tcount):
            volt[y, margin + t] = vol32[:, y, t * tile : (t + 1) * tile]

    def own_row(y):
        return volt[y, margin : margin + tcount].reshape(flat, tile)

    ys[0] = own_row(0).astype(BF16)
    ys[1] = own_row(rows - 1).astype(BF16)

    def send(src, dst, ssem, rsem, s, a):
        return pltpu.make_async_remote_copy(
            src_ref=src,
            dst_ref=dst,
            send_sem=ssem,
            recv_sem=rsem,
            device_id=(s, a),
            device_id_type=pl.DeviceIdType.MESH,
        )

    halos = (
        (has_ym, send(ys.at[0], yr.at[1], y_ssem.at[0], y_rsem.at[1], slab, me - 1)),
        (has_yp, send(ys.at[1], yr.at[0], y_ssem.at[1], y_rsem.at[0], slab, me + 1)),
        (has_zm, send(vol32.at[0], zr.at[1], z_ssem.at[0], z_rsem.at[1], slab - 1, me)),
        (has_zp, send(vol32.at[depth - 1], zr.at[0], z_ssem.at[1], z_rsem.at[0], slab + 1, me)),
        (has_down, send(vol32.at[0], cr.at[1], c_ssem.at[0], c_rsem.at[1], slab - 1, me + 1)),
        (has_up, send(vol32.at[depth - 1], cr.at[0], c_ssem.at[1], c_rsem.at[0], slab + 1, me - 1)),
    )
    arrivals = (
        (has_yp, yr.at[1], send(ys.at[0], yr.at[1], y_ssem.at[0], y_rsem.at[1], slab, me + 1)),
        (has_ym, yr.at[0], send(ys.at[1], yr.at[0], y_ssem.at[1], y_rsem.at[0], slab, me - 1)),
        (has_zp, zr.at[1], send(vol32.at[0], zr.at[1], z_ssem.at[0], z_rsem.at[1], slab + 1, me)),
        (has_zm, zr.at[0], send(vol32.at[depth - 1], zr.at[0], z_ssem.at[1], z_rsem.at[0], slab - 1, me)),
        (has_up, cr.at[1], send(vol32.at[0], cr.at[1], c_ssem.at[0], c_rsem.at[1], slab + 1, me - 1)),
        (has_down, cr.at[0], send(vol32.at[depth - 1], cr.at[0], c_ssem.at[1], c_rsem.at[0], slab - 1, me + 1)),
    )
    def starts(angle, y, sign):
        found = []
        for k in range(band):
            shift = off_ref[angle, first_row + y] + (k - center)
            used = cnt_ref[angle, first_row + y] > k
            found.append(jnp.where(used, margin + sign * shift, zero_start))
        return found

    def view(angle):
        pieces = []
        for y in range(rows):
            for start in starts(angle, y, 1):
                pieces.append(volt[y, pl.ds(start, tcount)].reshape(flat, tile).astype(BF16))
        weights = tiles[angle].reshape(rows * band * tile, tile)
        return jnp.dot(jnp.concatenate(pieces, axis=1), weights, preferred_element_type=F32)

    def sib_copy(i):
        return send(sib_send.at[i], sib_recv.at[i], sib_ssem.at[i], sib_rsem.at[i], slab, sib)

    part = flat // HALVES

    def span(h):
        return pl.ds(h * part, part)

    def chip_copy(i, h):
        return send(
            chip_send.at[i, span(h)],
            chip_recv.at[i, span(h)],
            chip_ssem.at[i, h],
            chip_rsem.at[i, h],
            slab,
            2 * dest[i] + core,
        )

    def for_sibling(i):
        loads[i][0].wait()
        sib_send[i] = view(2 * dest[i] + 1 - core)

    off_copy.wait()
    cnt_copy.wait()
    for_sibling(0)

    one = jnp.int32(1)
    none = jnp.int32(0)
    expect = jnp.int32(chips)
    for there in (has_far, has_zp, has_zm, has_up, has_down):
        expect = expect + jnp.where(there, one, none)
    pl.semaphore_wait(barrier, expect)

    sib_copy(0).start()
    for there, copy in halos:
        pl.when(there)(copy.start)

    for i in range(chips):
        if i + 1 < chips:
            for_sibling(i + 1)
            sib_copy(i + 1).start()
        loads[i][1].wait()
        part_own[...] = view(2 * dest[i] + core)
        sib_copy(i).wait_recv()
        if i + 1 < chips:
            chip_send[i] = part_own[...] + sib_recv[i]
            chip_copy(i, 0).start()
        else:
            part_own[...] = part_own[...] + sib_recv[i]

    for h in range(1, HALVES):
        for i in range(chips - 1):
            chip_copy(i, h).start()

    for there, buffer, copy in arrivals:
        pl.when(there)(copy.wait_recv)

        @pl.when(jnp.logical_not(there))
        def _(buffer=buffer):
            buffer[...] = jnp.zeros(buffer.shape, buffer.dtype)

    lane = lax.broadcasted_iota(jnp.int32, (flat + depth, tile), 1)
    level = lax.rem(lax.broadcasted_iota(jnp.int32, (flat + depth, tile), 0), depth)
    zeros_tile = jnp.zeros((depth, tile), F32)

    low = zr[0]
    low_y = jnp.concatenate([low[1:], cr[0][:1]], axis=0)
    low_lane = lax.broadcasted_iota(jnp.int32, (rows, width), 1)
    low_x = jnp.where(low_lane == width - 1, 0.0, pltpu.roll(low, width - 1, 1))
    lz, ly, lx = vol32[0] - low, low_y - low, low_x - low
    flow_low[...] = lz * lax.rsqrt(lz * lz + ly * ly + lx * lx + smooth_floor)

    def field_row(y):
        if 0 <= y < rows:
            return volt[y, margin - 1 : margin + tcount + 1].reshape(flat + 2 * depth, tile)
        inner = yr[0 if y < 0 else 1].astype(F32)
        return jnp.concatenate([zeros_tile, inner, zeros_tile], axis=0)

    def spread_row(ref, row):
        return [
            jnp.broadcast_to(ref[row : row + 1, t * tile : (t + 1) * tile], (depth, tile))
            for t in range(tcount)
        ]

    def flow(y):
        wide = field_row(y)
        here = wide[: flat + depth]
        rolled = pltpu.roll(wide, tile - 1, 1)
        dx = jnp.where(lane == tile - 1, rolled[depth:], rolled[: flat + depth]) - here
        dy = field_row(y + 1)[: flat + depth] - here
        top = spread_row(zr.at[1], y) if y >= 0 else spread_row(cr.at[1], rows - 1)
        top = jnp.concatenate([zeros_tile] + top, axis=0)
        dz = jnp.where(level == depth - 1, top, pltpu.roll(here, flat + depth - 1, 0)) - here
        inv = lax.rsqrt(dz * dz + dy * dy + dx * dx + smooth_floor)
        return dz * inv, dy * inv, dx * inv

    before = flow(-1)[1][depth:]
    for y in range(rows):
        fz, fy, fx = flow(y)
        fz, fy = fz[depth:], fy[depth:]
        under = jnp.concatenate(spread_row(flow_low, y), axis=0)
        div = fz - jnp.where(level[:flat] == 0, under, pltpu.roll(fz, 1, 0))
        div = div + (fy - before)
        rolled = pltpu.roll(fx, 1, 1)
        div = div + (fx[depth:] - jnp.where(lane[:flat] == 0, rolled[:flat], rolled[depth:]))
        base[y] = own_row(y) + step_size * smooth_weight * div
        before = fy

    def same_copy(i, h):
        return send(
            own_res.at[span(h)],
            same_recv.at[i, span(h)],
            same_ssem.at[i, h],
            same_rsem.at[i, h],
            slab,
            2 * dest[i] + core,
        )

    def forward(i, h):
        src = own_res.at[span(h)] if i == chips - 1 else same_recv.at[i, span(h)]
        return send(src, sibres_recv.at[i, span(h)], sr_ssem.at[i, h], sr_rsem.at[i, h], slab, sib)

    meas_copy.wait()
    for h in range(HALVES):
        total = part_own[span(h)]
        for i in range(chips - 1):
            chip_copy(i, h).wait_recv()
            total = total + chip_recv[i, span(h)]
        total = total.reshape(tcount // HALVES, depth, tile)
        first = h * (tcount // HALVES)
        for j in range(tcount // HALVES):
            t = first + j
            here = total[j] - meas[0, :, t * tile : (t + 1) * tile]
            res_ref[0, :, t * tile : (t + 1) * tile] = here
            respad[0, margin + t] = here.astype(BF16).astype(F32)
        block = respad[0, margin + first : margin + first + tcount // HALVES]
        own_res[span(h)] = block.reshape(part, tile).astype(BF16)
        for i in range(chips - 1):
            same_copy(i, h).start()
        forward(chips - 1, h).start()
    res_copy = pltpu.make_async_copy(res_ref, res_hbm, load_sem.at[n + 4])
    res_copy.start()

    def back(angle, slot, fresh):
        for y in range(rows):
            pieces = [
                respad[slot, pl.ds(start, tcount)].reshape(flat, tile).astype(BF16)
                for start in starts(angle, y, -1)
            ]
            weights = jnp.concatenate([tiles[angle, y, k] for k in range(band)], axis=1)
            acc = lax.dot_general(
                jnp.concatenate(pieces, axis=1),
                weights,
                (((1,), (1,)), ((), ())),
                preferred_element_type=F32,
            )
            grad[y] = acc if fresh else grad[y] + acc

    def take(block, slot):
        respad[slot, margin:zero_start] = block.astype(F32).reshape(tcount, depth, tile)

    def pass_on(i, h):
        same_copy(i, h).wait_recv()
        forward(i, h).start()

    def from_sibling(i):
        for h in range(HALVES):
            forward(i, h).wait_recv()
        take(sibres_recv[i], 1)
        back(2 * source[i] + 1 - core, 1, False)

    back(me, 0, True)
    for h in range(HALVES - 1):
        for i in range(chips - 1):
            pass_on(i, h)
    from_sibling(chips - 1)
    for i in range(chips - 1):
        pass_on(i, HALVES - 1)
        take(same_recv[i], 0)
        back(2 * source[i] + core, 0, False)
        if i > 0:
            from_sibling(i - 1)
    from_sibling(chips - 2)

    for y in range(rows):
        out = (base[y] - step_size * grad[y]).reshape(tcount, depth, tile)
        for t in range(tcount):
            upd_ref[:, y, t * tile : (t + 1) * tile] = out[t]
    upd_copy = pltpu.make_async_copy(upd_ref, upd_hbm, load_sem.at[n + 5])
    upd_copy.start()

    for there, copy in halos:
        pl.when(there)(copy.wait_send)
    for i in range(chips):
        sib_copy(i).wait_send()
        for h in range(HALVES):
            forward(i, h).wait_send()
            if i + 1 < chips:
                chip_copy(i, h).wait_send()
                same_copy(i, h).wait_send()
    res_copy.wait()
    upd_copy.wait()


def finish(upd_in, res_in, upd_out, res_out, upd, res, sem):
    parts = sem.shape[1] - 1
    size = upd.shape[0] // parts
    pairs = [(res_in, res, res_out)]
    for i in range(parts):
        span = pl.ds(i * size, size)
        pairs.append((upd_in.at[span], upd.at[span], upd_out.at[span]))
    reads = [pltpu.make_async_copy(p[0], p[1], sem.at[0, i]) for i, p in enumerate(pairs)]
    writes = [pltpu.make_async_copy(p[1], p[2], sem.at[1, i]) for i, p in enumerate(pairs)]
    for read in reads:
        read.start()
    for read, write in zip(reads, writes):
        read.wait()
        write.start()
    for write in writes:
        write.wait()


def per_device(slabs, n, volume, measured, ray_tiles, tile_offsets, band_counts):
    depth, rows, width = volume.shape
    count, unused, band, tile, unused_2 = ray_tiles.shape
    tcount = width // tile
    flat = tcount * depth
    padded = 2 * tcount + OFFMAX + band
    chips = n // 2
    dma = pltpu.SemaphoreType.DMA
    vmem = pltpu.VMEM
    block = (flat, tile)
    shapes = (
        jax.ShapeDtypeStruct(volume.shape, F32),
        jax.ShapeDtypeStruct(measured.shape, F32),
    )
    updated, residual = pl.pallas_call(
        functools.partial(kernel, slabs, n),
        out_shape=shapes,
        in_specs=[pl.BlockSpec(memory_space=pl.ANY)] * 5,
        out_specs=(pl.BlockSpec(memory_space=pl.ANY),) * 2,
        scratch_shapes=[
            vmem(volume.shape, F32),
            vmem(measured.shape, F32),
            vmem(volume.shape, BF16),
            vmem(measured.shape, F32),
            vmem(ray_tiles.shape, BF16),
            vmem(volume.shape, F32),
            vmem((rows, padded, depth, tile), F32),
            vmem(block, F32),
            vmem((chips, *block), F32),
            vmem((chips, *block), F32),
            vmem((chips - 1, *block), F32),
            vmem((chips - 1, *block), F32),
            vmem((chips - 1, *block), BF16),
            vmem((chips, *block), BF16),
            vmem(block, BF16),
            vmem((2, padded, depth, tile), F32),
            vmem((rows, *block), F32),
            vmem((rows, *block), F32),
            vmem((rows, width), F32),
            vmem((2, *block), BF16),
            vmem((2, *block), BF16),
            vmem((2, rows, width), F32),
            vmem((2, rows, width), F32),
            pltpu.SMEM(tile_offsets.shape, jnp.int32),
            pltpu.SMEM(band_counts.shape, jnp.int32),
            dma((6 + n,)),
            dma((chips,)),
            dma((chips,)),
            dma((chips - 1, HALVES)),
            dma((chips - 1, HALVES)),
            dma((chips - 1, HALVES)),
            dma((chips - 1, HALVES)),
            dma((chips, HALVES)),
            dma((chips, HALVES)),
            dma((2,)),
            dma((2,)),
            dma((2,)),
            dma((2,)),
            dma((2,)),
            dma((2,)),
        ],
        compiler_params=pltpu.CompilerParams(
            collective_id=0, has_side_effects=True, vmem_limit_bytes=60 * 1024 * 1024
        ),
        name="step",
    )(volume, measured, ray_tiles, tile_offsets, band_counts)
    return pl.pallas_call(
        finish,
        out_shape=shapes,
        in_specs=[pl.BlockSpec(memory_space=pl.ANY)] * 2,
        out_specs=(pl.BlockSpec(memory_space=pl.ANY),) * 2,
        scratch_shapes=[vmem(volume.shape, F32), vmem(measured.shape, F32), dma((2, 5))],
        compiler_params=pltpu.CompilerParams(vmem_limit_bytes=60 * 1024 * 1024),
        name="finish",
    )(updated, residual)


def solution(mesh):
    return jax.shard_map(
        functools.partial(per_device, mesh.shape["slab"], mesh.shape["angle"]),
        mesh=mesh,
        in_specs=(
            P("slab", "angle", None),
            P("angle", "slab", None),
            P(None, "angle", None, None, None),
            P(),
            P(),
        ),
        out_specs=(P("slab", "angle", None), P("angle", "slab", None)),
        check_vma=False,
    )
```
